256 devices in a mesh: ux: 4 (over y_hi, core), uy: 4 (over x), bond: 16 (over y_lo, z).
Axes of the slice: x: 4, y: 4 (y_hi: 2, y_lo: 2; y = y_hi * 2 + y_lo), z: 8, core: 2. Of those that a mesh axis runs over, the one named last changes fastest.
Arguments:
- corner_up: bfloat16 [4, 4, 768, 768], P('ux', 'uy', 'bond'), may hold values from -6 to 6
- edge_top: bfloat16 [4, 4, 768, 4, 768], P('ux', 'uy', 'bond'), may hold values from -0.21875 to 0.21875
- edge_left: bfloat16 [4, 4, 768, 4, 768], P('ux', 'uy', 'bond'), may hold values from -6 to 6
- corner_down: bfloat16 [4, 4, 768, 768], P('ux', 'uy', 'bond'), may hold values from -6 to 6
- edge_bottom: bfloat16 [4, 4, 768, 4, 768], P('ux', 'uy', 'bond'), may hold values from -0.3125 to 0.3125
- site_weights: bfloat16 [4, 4, 4, 4, 4, 4], P('ux', 'uy'), may hold values from -3 to 3
- proj_upper: bfloat16 [4, 4, 768, 4, 768], P('ux', 'uy', 'bond'), may hold values from -0.109375 to 0.109375
- proj_lower: bfloat16 [4, 4, 768, 4, 768], P('ux', 'uy', 'bond'), may hold values from -0.15625 to 0.15625
Outputs:
- new_corner_up: bfloat16 [4, 4, 768, 768], P('ux', 'uy', 'bond')
- new_edge_left: bfloat16 [4, 4, 768, 4, 768], P('ux', 'uy', 'bond')
- new_corner_down: bfloat16 [4, 4, 768, 768], P('ux', 'uy', 'bond')
The draws below stay inside these ranges and needn't reach their ends.
All inputs are finite; a program needn't handle non-finite values.
Results may differ from the reference program's by a relative error of at most 0.0058.
Values may be sent and summed in bfloat16 or wider, within the bound.
A program may use at most 128 MiB of HBM per device.

```python
import jax
import jax.numpy as jnp
from jax import lax

CHI = 768
D = 4
LX = 4
LY = 4


def strengthened(values, rng, source, target, parts, factor):
    def block_of(position):
        return (jnp.arange(values.shape[position]) // (values.shape[position] // parts)).reshape((-1,) + (1,) * (values.ndim - 1 - position))

    one_side = jax.random.permutation(rng, parts)[block_of(target)]
    second = (block_of(target) + parts // 2) % parts
    return jnp.where((block_of(source) == one_side) | (block_of(source) == second), factor * values, values)


def shard_levels(rng, extent, shards, smallest, high):
    def one(axis_at, parts):
        steps = jax.random.uniform(jax.random.fold_in(jax.random.fold_in(rng, 6), axis_at), (parts,), jnp.float32, smallest / len(shards), high / len(shards))
        return jnp.repeat(jnp.exp(steps), extent[axis_at] // parts).reshape((-1,) + (1,) * (len(extent) - axis_at - 1))

    gain = one(*shards[0])
    for cut in shards[1:]:
        gain = gain * one(*cut)
    return gain


def bell_draw(own_key, dims, spread, bound, cuts=(), kind=jnp.bfloat16):
    loudness = shard_levels(own_key, dims, cuts, -0.22, 0.18) if cuts else 1.0
    values = jax.random.normal(own_key, dims, jnp.float32) * spread * loudness
    return jnp.minimum(jnp.maximum(values, -bound), bound).astype(kind)


def gaussian_with(own_key, shape, deviation, bound, split, heavy, held_as=jnp.bfloat16):
    array = deviation * jax.random.normal(own_key, shape, jnp.float32)
    if split:
        array = array * shard_levels(own_key, shape, split, -0.22, 0.18)
    return jnp.clip(strengthened(array, jax.random.fold_in(own_key, 3), *heavy), -bound, bound).astype(held_as)


def setup_inputs(seed: int = 0) -> dict:
    streams_of = jax.random.split(jax.random.key(seed), 9)
    corner_up = bell_draw(streams_of[0], (LX, LY, CHI, CHI), 1.0, 6.0, ((0, 4), (1, 4), (2, 16)))
    edge_top = bell_draw(streams_of[1], (LX, LY, CHI, D, CHI), CHI ** -0.5, 0.21875, ((0, 4), (1, 4), (2, 16)))
    edge_left = bell_draw(streams_of[2], (LX, LY, CHI, D, CHI), 1.0, 6.0, ((0, 4), (1, 4), (2, 16)))
    corner_down = bell_draw(streams_of[3], (LX, LY, CHI, CHI), 1.0, 6.0, ((0, 4), (1, 4), (2, 16)))
    edge_bottom = gaussian_with(streams_of[4], (LX, LY, CHI, D, CHI), CHI ** -0.5, 0.3125, ((0, 4), (1, 4), (2, 16)), (2, 4, 16, 2.0))
    site_weights = bell_draw(streams_of[5], (LX, LY, D, D, D, D), D ** -0.5, 3.0, ((0, 4), (1, 4)))
    proj_upper = bell_draw(streams_of[6], (LX, LY, CHI, D, CHI), (CHI * D) ** -0.5, 0.109375, ((0, 4), (1, 4), (2, 16)))
    proj_lower = gaussian_with(streams_of[7], (LX, LY, CHI, D, CHI), (CHI * D) ** -0.5, 0.15625, ((0, 4), (1, 4), (2, 16)), (2, 4, 16, 2.0))
    return dict(corner_up=corner_up, edge_top=edge_top, edge_left=edge_left, corner_down=corner_down, edge_bottom=edge_bottom, site_weights=site_weights, proj_upper=proj_upper, proj_lower=proj_lower)


def to_wide(values):
    return values.astype(jnp.float32)


def absorb_site(tensors):
    corner, top_edge, left_edge, low_corner, bottom_edge, weights, upper_proj, lower_proj = tensors
    enlarged = jnp.einsum('ab,ekb->ake', to_wide(corner), to_wide(top_edge)).astype(jnp.bfloat16)
    fresh_corner = jnp.einsum('akq,ake->qe', to_wide(lower_proj), to_wide(enlarged)).astype(jnp.bfloat16)
    stacked = jnp.einsum('alc,lurd->aurdc', to_wide(left_edge), to_wide(weights)).astype(jnp.bfloat16)
    framed = jnp.einsum('aurdc,cdq->aurq', to_wide(stacked), to_wide(upper_proj)).astype(jnp.bfloat16)
    fresh_edge = jnp.einsum('auq,aurc->qrc', to_wide(lower_proj), to_wide(framed)).astype(jnp.bfloat16)
    lowered = jnp.einsum('dc,ckq->dkq', to_wide(low_corner), to_wide(upper_proj)).astype(jnp.bfloat16)
    fresh_lower = jnp.einsum('dke,dkq->eq', to_wide(bottom_edge), to_wide(lowered)).astype(jnp.bfloat16)
    return fresh_corner, fresh_edge, fresh_lower


def flatten_cell(tensor):
    return tensor.reshape((LX * LY,) + tensor.shape[2:])


def restore_cell(tensor):
    return jnp.roll(tensor.reshape((LX, LY) + tensor.shape[1:]), 1, axis=0)


def reference(corner_up, edge_top, edge_left, corner_down, edge_bottom, site_weights, proj_upper, proj_lower):
    prev_lower = jnp.roll(proj_lower, 1, axis=1)
    inputs = tuple(flatten_cell(tensor) for tensor in (corner_up, edge_top, edge_left, corner_down, edge_bottom, site_weights, proj_upper, prev_lower))
    fresh = lax.map(absorb_site, inputs)
    return (restore_cell(fresh[0]), restore_cell(fresh[1]), restore_cell(fresh[2]))
```

```python
import jax
import jax.numpy as jnp
import numpy as np
from jax import lax
from jax.experimental import pallas as pl
from jax.experimental.pallas import tpu as pltpu
from jax.sharding import PartitionSpec as P

MESH = pl.DeviceIdType.MESH
BF = jnp.bfloat16
F32 = jnp.float32
ZN = 8
YN = 2
D = 4
CHI = 768
BLK = CHI // (ZN * YN)
HALF = CHI // YN
ROWS = D * BLK
SLABS = 6
COPIES = 96


def mul(a, b, ca=1, cb=0):
    return lax.dot_general(a, b, (((ca,), (cb,)), ((), ())), preferred_element_type=F32)


def kernel(
    pu, pl_, el, et, eb, cu, cd, w, mask, expand,
    out,
    pug, etg, elb, plb, ebb, cub, cdb, mix, xb, fb, lb, ebuf, outp, sbuf, rbuf, fin,
    ssem, rsem, lsem,
):
    bond = lax.axis_index("bond")
    ux = lax.axis_index("ux")
    uy = lax.axis_index("uy")
    yl = lax.div(bond, ZN)
    z = lax.rem(bond, ZN)
    yo = 1 - yl

    def dev(dz=0, other=False, dx=0, dy=0):
        bz = lax.rem(z + (dz + ZN), ZN)
        return (
            lax.rem(ux + (dx + 4), 4),
            lax.rem(uy + (dy + 4), 4),
            (yo if other else yl) * ZN + bz,
        )

    right, left, mate = dev(1), dev(-1), dev(other=True)

    barrier = pltpu.get_barrier_semaphore()
    sources = [left, right, mate, dev(dy=-1), dev(dy=-1, other=True), dev(dx=-1), dev(dx=-1, other=True)]
    for source in sources:
        pl.semaphore_signal(barrier, inc=1, device_id=source, device_id_type=MESH)
    pl.semaphore_wait(barrier, len(sources))

    started = []
    count = [0]

    def rcopy(src, dst, to):
        index = count[0]
        count[0] += 1
        copy = pltpu.make_async_remote_copy(
            src_ref=src, dst_ref=dst, send_sem=ssem.at[index], recv_sem=rsem.at[index],
            device_id=to, device_id_type=MESH,
        )
        copy.start()
        started.append(copy)
        return copy

    def zmod(k):
        return lax.rem(z + (k + ZN), ZN)

    def rows_c(half, zz):
        return pl.ds(pl.multiple_of(half * HALF + zz * BLK, 16), BLK)

    y_pu = rcopy(pu.at[yo], pug.at[:, rows_c(yl, z), :], mate)
    pr = {}
    pr_l = {}
    pr["own", 1] = rcopy(pu.at[yl], pug.at[:, rows_c(yl, z), :], right)
    pr_l["own", 1] = rcopy(pu.at[yl], pug.at[:, rows_c(yl, z), :], left)
    my192 = pl.ds(pl.multiple_of(yl * ROWS, 16), ROWS)
    my48 = pl.ds(pl.multiple_of(yl * BLK, 16), BLK)
    y_el = rcopy(el, elb.at[my192, :], mate)
    x_same = rcopy(pl_, plb.at[my192, :], dev(dy=1))
    x_other = rcopy(pl_, plb.at[my192, :], dev(dy=1, other=True))
    y_cd = rcopy(cd, cdb.at[my48, :], mate)
    y_cu = rcopy(cu, cub.at[my48, :], mate)
    y_eb = rcopy(eb, ebb.at[my192, :], mate)
    local = [
        (pu.at[yl], pug.at[:, rows_c(yl, z), :]),
        (et, etg.at[:, pl.ds(pl.multiple_of(z * BLK, 16), BLK), :]),
        (el, elb.at[my192, :]),
        (eb, ebb.at[my192, :]),
        (cu, cub.at[my48, :]),
        (cd, cdb.at[my48, :]),
    ]
    here = []
    for i, (src, dst) in enumerate(local):
        copy = pltpu.make_async_copy(src, dst, lsem.at[i])
        copy.start()
        here.append(copy)

    spread = mul(expand[...], w[...], 0, 0).astype(BF)
    mix[...] = (mul(spread, expand[...]) * mask[...].astype(F32)).astype(BF)

    def pu_at(half, zz):
        return pug.at[:, rows_c(half, zz), :]

    y_pu.wait_recv()
    pr["oth", 1] = rcopy(pu_at(yo, z), pu_at(yo, z), right)
    pr_l["oth", 1] = rcopy(pu_at(yo, z), pu_at(yo, z), left)

    def forward_pu(m):
        for name, half in (("own", yl), ("oth", yo)):
            if (name, m) in pr:
                pr[name, m].wait_recv()
                if m < 3 or (m == 3 and name == "own"):
                    at = pu_at(half, zmod(-m))
                    pr[name, m + 1] = rcopy(at, at, right)
            if (name, m) in pr_l:
                pr_l[name, m].wait_recv()
                if m < 3 or (m == 3 and name == "oth"):
                    at = pu_at(half, zmod(m))
                    pr_l[name, m + 1] = rcopy(at, at, left)

    er = {}
    er_l = {}

    def et_at(part, zz):
        return etg.at[pl.ds(part * 2, 2), pl.ds(pl.multiple_of(zz * BLK, 16), BLK), :]

    def forward_et(m):
        for part in (0, 1):
            if (part, m) in er:
                er[part, m].wait_recv()
                if m < 3 or (m == 3 and part == 0):
                    at = et_at(part, zmod(-m))
                    er[part, m + 1] = rcopy(at, at, right)
            if (part, m) in er_l:
                er_l[part, m].wait_recv()
                if m < 3 or (m == 3 and part == 1):
                    at = et_at(part, zmod(m))
                    er_l[part, m + 1] = rcopy(at, at, left)

    forward_pu(1)
    forward_pu(2)
    for part in (0, 1):
        er[part, 1] = rcopy(et.at[pl.ds(part * 2, 2)], et_at(part, z), right)
        er_l[part, 1] = rcopy(et.at[pl.ds(part * 2, 2)], et_at(part, z), left)
    forward_pu(3)
    forward_pu(4)

    for copy in here:
        copy.wait()
    y_el.wait_recv()
    y_cd.wait_recv()

    def x_step(d, carry):
        x = mul(elb[...], pug[d]).astype(BF)
        base = pl.multiple_of(d * ROWS, 16)
        xb[0, pl.ds(base, ROWS), :] = x[:ROWS]
        xb[1, pl.ds(base, ROWS), :] = x[ROWS:]
        low = mul(cdb[...], pug[d]).astype(BF)
        base = pl.multiple_of(d * BLK, 16)
        lb[pl.ds(base, BLK), :] = low[:BLK]
        lb[pl.ds(pl.multiple_of(ROWS + d * BLK, 16), BLK), :] = low[BLK:]
        return carry

    lax.fori_loop(0, D, x_step, 0)
    forward_et(1)

    def mix_step(h, carry):
        f = mul(mix[...], xb[h]).astype(BF)
        for r in range(D):
            fb[r, pl.ds(pl.multiple_of(h * ROWS, 16), ROWS), :] = f[r * ROWS:(r + 1) * ROWS]
        return carry

    lax.fori_loop(0, YN, mix_step, 0)
    x_same.wait_recv()
    x_other.wait_recv()
    y_eb.wait_recv()
    y_cu.wait_recv()

    def edge_step(r, carry):
        outp[r] = mul(plb[...], fb[r], 0, 0)
        return carry

    lax.fori_loop(0, D, edge_step, 0)
    outp[4] = mul(ebb[...], lb[...], 0, 0)
    forward_et(2)

    def own(j0, n, h, zz):
        return outp[j0:j0 + n, pl.ds(pl.multiple_of(h * HALF + zz * BLK, 16), BLK), :]

    flows = {}

    def rs_first(j0, n):
        zz = zmod(4)
        for side, h, to in ((0, 0, right), (1, 1, left)):
            sbuf[side, 0, h, j0:j0 + n] = own(j0, n, h, zz).astype(BF)
            flows[j0, side, 1] = rcopy(
                sbuf.at[side, 0, h, pl.ds(j0, n)], rbuf.at[side, 0, h, pl.ds(j0, n)], to
            )

    def rs_next(j0, n, t):
        for side, sign, to in ((0, 1, right), (1, -1, left)):
            flows[j0, side, t - 1].wait_recv()
            zz = zmod(sign * (5 - t))
            for h in range(YN):
                value = own(j0, n, h, zz)
                if t > 2 or h == side:
                    value = value + rbuf[side, t - 2, h, j0:j0 + n].astype(F32)
                sbuf[side, t - 1, h, j0:j0 + n] = value.astype(BF)
            flows[j0, side, t] = rcopy(
                sbuf.at[side, t - 1, :, pl.ds(j0, n)], rbuf.at[side, t - 1, :, pl.ds(j0, n)], to
            )

    outs = []

    def rs_last(j0, n):
        for side in range(2):
            flows[j0, side, 4].wait_recv()
        for h in range(YN):
            value = own(j0, n, h, z)
            for side in range(2):
                value = value + rbuf[side, 3, h, j0:j0 + n].astype(F32)
            fin[h, j0:j0 + n] = value.astype(BF)
        outs.append(rcopy(fin.at[yl, pl.ds(j0, n)], out.at[yl, pl.ds(j0, n)], dev(dx=1)))
        outs.append(rcopy(fin.at[yo, pl.ds(j0, n)], out.at[yl, pl.ds(j0, n)], dev(dx=1, other=True)))

    waves = [(0, 2), (2, 2), (4, 1)]
    for j0, n in waves:
        rs_first(j0, n)
    forward_et(3)
    for j0, n in waves:
        rs_next(j0, n, 2)
    forward_et(4)

    def corner_step(k, carry):
        part = mul(cub[...], etg[k], 1, 1).astype(BF)
        ebuf[pl.ds(pl.multiple_of(k * BLK, 16), BLK), :] = part[:BLK]
        ebuf[pl.ds(pl.multiple_of(ROWS + k * BLK, 16), BLK), :] = part[BLK:]
        return carry

    lax.fori_loop(0, D, corner_step, 0)
    outp[5] = mul(plb[...], ebuf[...], 0, 0)
    rs_first(5, 1)
    for j0, n in waves:
        rs_next(j0, n, 3)
    rs_next(5, 1, 2)
    for j0, n in waves:
        rs_next(j0, n, 4)
    rs_next(5, 1, 3)
    rs_next(5, 1, 4)
    for j0, n in waves:
        rs_last(j0, n)
    rs_last(5, 1)
    for copy in outs:
        copy.wait_recv()
    for copy in started:
        copy.wait_send()


def constants():
    index = np.arange(D * D * BLK)
    mask = (index[:, None] % BLK == index[None, :] % BLK).astype(np.float32)
    expand = (np.arange(D * D)[:, None] == index[None, :] // BLK).astype(np.float32)
    return jnp.asarray(mask, BF), jnp.asarray(expand, BF)


def shards(
    corner_up, edge_top, edge_left, corner_down, edge_bottom, site_weights, proj_upper, proj_lower
):
    def rows(t):
        return t[0, 0].transpose(1, 0, 2)

    pu = proj_upper[0, 0].reshape(BLK, D, YN, HALF).transpose(2, 1, 0, 3)
    low = rows(proj_lower).reshape(ROWS, CHI)
    el = rows(edge_left).reshape(ROWS, CHI)
    et = rows(edge_top)
    eb = rows(edge_bottom).reshape(ROWS, CHI)
    w = site_weights[0, 0].transpose(2, 1, 3, 0).reshape(D * D, D * D)
    mask, expand = constants()
    vmem = pl.BlockSpec(memory_space=pltpu.VMEM)
    rows2 = YN * ROWS
    out = pl.pallas_call(
        kernel,
        out_shape=jax.ShapeDtypeStruct((YN, SLABS, BLK, HALF), BF),
        in_specs=[vmem] * 10,
        out_specs=vmem,
        scratch_shapes=[
            pltpu.VMEM((D, CHI, HALF), BF),
            pltpu.VMEM((D, HALF, CHI), BF),
            pltpu.VMEM((rows2, CHI), BF),
            pltpu.VMEM((rows2, CHI), BF),
            pltpu.VMEM((rows2, CHI), BF),
            pltpu.VMEM((YN * BLK, CHI), BF),
            pltpu.VMEM((YN * BLK, CHI), BF),
            pltpu.VMEM((D * ROWS, D * ROWS), BF),
            pltpu.VMEM((YN, D * ROWS, HALF), BF),
            pltpu.VMEM((D, rows2, HALF), BF),
            pltpu.VMEM((rows2, HALF), BF),
            pltpu.VMEM((rows2, HALF), BF),
            pltpu.VMEM((SLABS, CHI, HALF), F32),
            pltpu.VMEM((2, 4, YN, SLABS, BLK, HALF), BF),
            pltpu.VMEM((2, 4, YN, SLABS, BLK, HALF), BF),
            pltpu.VMEM((YN, SLABS, BLK, HALF), BF),
            pltpu.SemaphoreType.DMA((COPIES,)),
            pltpu.SemaphoreType.DMA((COPIES,)),
            pltpu.SemaphoreType.DMA((8,)),
        ],
        compiler_params=pltpu.CompilerParams(
            collective_id=0, has_side_effects=True, vmem_limit_bytes=56 * 1024 * 1024
        ),
    )(pu, low, el, et, eb, corner_up[0, 0], corner_down[0, 0], w, mask, expand)
    edge = out[:, :D].transpose(2, 1, 0, 3).reshape(1, 1, BLK, D, CHI)
    lower = out[:, D].transpose(1, 0, 2).reshape(1, 1, BLK, CHI)
    upper = out[:, D + 1].transpose(1, 0, 2).reshape(1, 1, BLK, CHI)
    return upper, edge, lower


def solution(mesh):
    return jax.shard_map(
        shards,
        mesh=mesh,
        in_specs=(
            P("ux", "uy", "bond", None),
            P("ux", "uy", "bond", None, None),
            P("ux", "uy", "bond", None, None),
            P("ux", "uy", "bond", None),
            P("ux", "uy", "bond", None, None),
            P("ux", "uy", None, None, None, None),
            P("ux", "uy", "bond", None, None),
            P("ux", "uy", "bond", None, None),
        ),
        out_specs=(
            P("ux", "uy", "bond", None),
            P("ux", "uy", "bond", None, None),
            P("ux", "uy", "bond", None),
        ),
        check_vma=False,
    )
```

```python
import jax
import jax.numpy as jnp
from jax import lax
from jax.experimental import pallas as pl
from jax.experimental.pallas import tpu as pltpu
from jax.sharding import PartitionSpec as P

MESH = pl.DeviceIdType.MESH
BF = jnp.bfloat16
F32 = jnp.float32
ZN = 8
YN = 2
D = 4
CHI = 768
BLK = CHI // (ZN * YN)
HALF = CHI // YN
ROWS = D * BLK
SLABS = 6
COPIES = 96


def mul(a, b, ca=1, cb=0):
    return lax.dot_general(a, b, (((ca,), (cb,)), ((), ())), preferred_element_type=F32)


def kernel(
    pu, low, el, et, eb, cu, cd, w,
    out,
    put, pug, cug, etb, elb, plb, lpb, ebb, cdb, mix, xb, fb, lb, pick, e2, er, ebuf, outp, sbuf, rbuf, fin,
    ssem, rsem, asem, bsem, lsem,
):
    bond = lax.axis_index("bond")
    ux = lax.axis_index("ux")
    uy = lax.axis_index("uy")
    yl = lax.div(bond, ZN)
    z = lax.rem(bond, ZN)
    yo = 1 - yl
    zh = lax.div(z, ZN // 2)
    zq = lax.rem(z, ZN // 2)

    def zmod(k):
        return lax.rem(z + (k + ZN), ZN)

    def at_bond(half, zz, dx=0, dy=0):
        return (lax.rem(ux + (dx + 4), 4), lax.rem(uy + (dy + 4), 4), half * ZN + zz)

    right, left, mate = at_bond(yl, zmod(1)), at_bond(yl, zmod(-1)), at_bond(yo, z)

    barrier = pltpu.get_barrier_semaphore()
    sources = [
        left, right, mate,
        at_bond(yl, z, dy=-1), at_bond(yo, z, dy=-1), at_bond(yl, z, dx=-1), at_bond(yo, z, dx=-1),
    ]

    def greet(to):
        pl.semaphore_signal(barrier, inc=1, device_id=to, device_id_type=MESH)

    for source in sources:
        greet(source)
    for half in range(YN):
        for q in range(ZN // 2):
            zz = yl * (ZN // 2) + q

            @pl.when(half * ZN + zz != bond)
            def _():
                greet(at_bond(half, zz))

    turned = jnp.transpose(pu[...], (1, 0, 2))
    put[0] = turned[:, :, :HALF]
    put[1] = turned[:, :, HALF:]
    pl.semaphore_wait(barrier, len(sources) + ZN - jnp.where(zh == yl, 1, 0))

    started = []
    count = [0]

    def rcopy(src, dst, to):
        index = count[0]
        count[0] += 1
        copy = pltpu.make_async_remote_copy(
            src_ref=src, dst_ref=dst, send_sem=ssem.at[index], recv_sem=rsem.at[index],
            device_id=to, device_id_type=MESH,
        )
        copy.start()
        started.append(copy)
        return copy

    def rows_c(half, zz):
        return pl.ds(pl.multiple_of(half * HALF + zz * BLK, 16), BLK)

    def rows_z(zz):
        return pl.ds(pl.multiple_of(zz * BLK, 16), BLK)

    my192 = pl.ds(pl.multiple_of(yl * ROWS, 16), ROWS)
    my48 = pl.ds(pl.multiple_of(yl * BLK, 16), BLK)

    def pu_at(half, zz):
        return pug.at[:, rows_c(half, zz), :]

    def cu_at(zz, part=None):
        if part is None:
            return cug.at[rows_z(zz), :]
        return cug.at[rows_z(zz), pl.ds(part * HALF, HALF)]

    pr, ql = {}, {}
    pr["own", 1] = rcopy(put.at[yl], pu_at(yl, z), right)
    ql["own", 1] = rcopy(put.at[yl], pu_at(yl, z), left)
    y_pu = rcopy(put.at[yo], pu_at(yl, z), mate)
    pr["cu", 1] = rcopy(cu, cu_at(z), right)
    ql["cu", 1] = rcopy(cu, cu_at(z), left)
    here = []
    for i, (src, dst) in enumerate([(put.at[yl], pu_at(yl, z)), (cu, cu_at(z)), (cd, cdb.at[my48, :])]):
        copy = pltpu.make_async_copy(src, dst, lsem.at[i])
        copy.start()
        here.append(copy)
    etb[:, yl] = jnp.transpose(et[...], (1, 0, 2))
    y_et = rcopy(etb.at[:, yl], etb.at[:, yl], mate)
    plb[my192, :] = jnp.transpose(low[...], (1, 0, 2)).reshape(ROWS, CHI)
    x_same = rcopy(plb.at[my192, :], lpb.at[my192, :], at_bond(yl, z, dy=1))
    x_other = rcopy(plb.at[my192, :], lpb.at[my192, :], at_bond(yo, z, dy=1))
    y_pu.wait_recv()
    pr["oth", 1] = rcopy(pu_at(yo, z), pu_at(yo, z), right)
    ql["oth", 1] = rcopy(pu_at(yo, z), pu_at(yo, z), left)
    elb[my192, :] = jnp.transpose(el[...], (1, 0, 2)).reshape(ROWS, CHI)
    y_el = rcopy(elb.at[my192, :], elb.at[my192, :], mate)
    y_cd = rcopy(cd, cdb.at[my48, :], mate)
    ebb[my192, :] = jnp.transpose(eb[...], (1, 0, 2)).reshape(ROWS, CHI)
    y_eb = rcopy(ebb.at[my192, :], ebb.at[my192, :], mate)

    def forward(name, m):
        for flow, sign, to, last in ((pr, -1, right, "own"), (ql, 1, left, "oth")):
            if (name, m) not in flow:
                continue
            flow[name, m].wait_recv()
            zz = zmod(sign * m)
            if name == "cu":
                if m < 4:
                    at = cu_at(zz) if m < 3 else cu_at(zz, 0 if last == "own" else 1)
                    flow[name, m + 1] = rcopy(at, at, to)
            elif m < 3 or (m == 3 and name == last):
                at = pu_at(yl if name == "own" else yo, zz)
                flow[name, m + 1] = rcopy(at, at, to)

    forward("own", 1)
    forward("cu", 1)
    size = D * D * BLK
    rowi = lax.broadcasted_iota(jnp.int32, (size, D ** 3), 0)
    coli = lax.broadcasted_iota(jnp.int32, (size, D ** 3), 1)
    legs = lax.rem(lax.div(rowi, BLK), D) * D + lax.div(rowi, ROWS)
    weights = w[...].reshape(D ** 3, D)
    spread = jnp.zeros((size, D * D), F32)
    for l in range(D):
        one = jnp.where(coli == legs + l * D * D, 1.0, 0.0).astype(BF)
        d_at = lax.broadcasted_iota(jnp.int32, (D, D * D), 0) * D + l
        col = lax.broadcasted_iota(jnp.int32, (D, D * D), 1)
        spread = spread + mul(mul(one, weights).astype(BF), jnp.where(col == d_at, 1.0, 0.0).astype(BF))
    leg = lax.broadcasted_iota(jnp.int32, (D * D, size), 0)
    pos = lax.broadcasted_iota(jnp.int32, (D * D, size), 1)
    expand = jnp.where(leg == lax.div(pos, BLK), 1.0, 0.0).astype(BF)
    full = mul(spread.astype(BF), expand)
    inrow = lax.rem(lax.broadcasted_iota(jnp.int32, (size, 1), 0), BLK)
    incol = lax.rem(lax.broadcasted_iota(jnp.int32, (1, size), 1), BLK)
    mix[...] = jnp.where(inrow == incol, full, 0.0).astype(BF)

    forward("oth", 1)
    forward("cu", 2)
    forward("own", 2)
    forward("oth", 2)
    lane = lax.broadcasted_iota(jnp.int32, (1, HALF), 1)
    upper = jnp.where(lane >= ROWS, 1, 0)
    rest = lane - upper * ROWS
    target = 3 * 2 * BLK + upper * BLK + rest + lax.div(rest, BLK) * (HALF - BLK)
    pick[...] = jnp.where(
        lax.broadcasted_iota(jnp.int32, pick.shape, 0) == target, 1.0, 0.0
    ).astype(BF)

    forward("cu", 3)
    forward("own", 3)
    forward("oth", 3)
    for copy in here:
        copy.wait()
    y_et.wait_recv()
    forward("cu", 4)
    e2[...] = mul(cug[...], etb[...].reshape(HALF, CHI), 1, 1).astype(BF).reshape(ZN, BLK, HALF)

    def er_at(half, q):
        return er.at[half, :, pl.ds(pl.multiple_of(q * HALF, 128), HALF)]

    slot = yl * (ZN // 2) + zq

    def exchange(dz):
        return pltpu.make_async_remote_copy(
            src_ref=e2.at[zmod(dz)], dst_ref=er_at(yl, zq), send_sem=asem.at[dz], recv_sem=bsem.at[slot],
            device_id=at_bond(zh, zmod(dz)), device_id_type=MESH,
        )

    for dz in (4, 3, 5, 2, 6, 1, 7):
        exchange(dz).start()

    @pl.when(zh == yl)
    def _():
        pltpu.make_async_copy(e2.at[z], er_at(yl, zq), bsem.at[slot]).start()

    @pl.when(zh != yl)
    def _():
        exchange(0).start()

    forward("own", 4)
    forward("oth", 4)
    y_el.wait_recv()
    y_cd.wait_recv()

    def x_step(d, carry):
        x = mul(elb[...], pug[d]).astype(BF)
        base = pl.multiple_of(d * ROWS, 16)
        xb[0, pl.ds(base, ROWS), :] = x[:ROWS]
        xb[1, pl.ds(base, ROWS), :] = x[ROWS:]
        return carry

    lax.fori_loop(0, D, x_step, 0)

    def mix_step(h, carry):
        f = mul(mix[...], xb[h]).astype(BF)
        for r in range(D):
            fb[r, pl.ds(pl.multiple_of(h * ROWS, 16), ROWS), :] = f[r * ROWS:(r + 1) * ROWS]
        return carry

    lax.fori_loop(0, YN, mix_step, 0)
    x_same.wait_recv()
    x_other.wait_recv()

    def edge_step(r, carry):
        outp[r] = mul(lpb[...], fb[r], 0, 0)
        return carry

    def own(j0, n, h, zz):
        return outp[j0:j0 + n, pl.ds(pl.multiple_of(h * HALF + zz * BLK, 16), BLK), :]

    flows = {}

    def rs_first(j0, n):
        zz = zmod(4)
        for side, h, to in ((0, 0, right), (1, 1, left)):
            sbuf[side, 0, h, j0:j0 + n] = own(j0, n, h, zz).astype(BF)
            flows[j0, side, 1] = rcopy(
                sbuf.at[side, 0, h, pl.ds(j0, n)], rbuf.at[side, 0, h, pl.ds(j0, n)], to
            )

    def rs_next(j0, n, t):
        for side, sign, to in ((0, 1, right), (1, -1, left)):
            flows[j0, side, t - 1].wait_recv()
            zz = zmod(sign * (5 - t))
            for h in range(YN):
                value = own(j0, n, h, zz)
                if t > 2 or h == side:
                    value = value + rbuf[side, t - 2, h, j0:j0 + n].astype(F32)
                sbuf[side, t - 1, h, j0:j0 + n] = value.astype(BF)
            flows[j0, side, t] = rcopy(
                sbuf.at[side, t - 1, :, pl.ds(j0, n)], rbuf.at[side, t - 1, :, pl.ds(j0, n)], to
            )

    outs = []

    def rs_last(j0, n):
        for side in range(2):
            flows[j0, side, 4].wait_recv()
        for h in range(YN):
            value = own(j0, n, h, z)
            for side in range(2):
                value = value + rbuf[side, 3, h, j0:j0 + n].astype(F32)
            fin[h, j0:j0 + n] = value.astype(BF)
        outs.append(rcopy(fin.at[yl, pl.ds(j0, n)], out.at[yl, pl.ds(j0, n)], at_bond(yl, z, dx=1)))
        outs.append(rcopy(fin.at[yo, pl.ds(j0, n)], out.at[yl, pl.ds(j0, n)], at_bond(yo, z, dx=1)))

    waves = [(0, 2), (2, 2), (4, 1), (5, 1)]
    lax.fori_loop(0, 2, edge_step, 0)
    rs_first(0, 2)
    lax.fori_loop(2, 4, edge_step, 0)
    rs_first(2, 2)

    def low_step(d, carry):
        part = mul(cdb[...], pug[d]).astype(BF)
        lb[pl.ds(pl.multiple_of(d * BLK, 16), BLK), :] = part[:BLK]
        lb[pl.ds(pl.multiple_of(ROWS + d * BLK, 16), BLK), :] = part[BLK:]
        return carry

    lax.fori_loop(0, D, low_step, 0)
    y_eb.wait_recv()
    outp[4] = mul(ebb[...], lb[...], 0, 0)
    rs_first(4, 1)
    rs_next(0, 2, 2)
    for half in range(YN):
        for q in range(ZN // 2):
            pltpu.make_async_copy(e2.at[0], er_at(half, q), bsem.at[half * (ZN // 2) + q]).wait()

    def pick_step(k, carry):
        shift = pl.multiple_of((3 - k) * 2 * BLK, 16)
        part = mul(er[...].reshape(YN * BLK, 4 * HALF), pick[pl.ds(shift, 4 * HALF), :]).astype(BF)
        ebuf[pl.ds(pl.multiple_of(k * BLK, 16), BLK), :] = part[:BLK]
        ebuf[pl.ds(pl.multiple_of(ROWS + k * BLK, 16), BLK), :] = part[BLK:]
        return carry

    lax.fori_loop(0, D, pick_step, 0)
    outp[5] = mul(lpb[...], ebuf[...], 0, 0)
    rs_first(5, 1)
    for j0, n in waves[1:]:
        rs_next(j0, n, 2)
    for t in (3, 4):
        for j0, n in waves:
            rs_next(j0, n, t)
    for j0, n in waves:
        rs_last(j0, n)
    for copy in outs:
        copy.wait_recv()
    for copy in started:
        copy.wait_send()
    for dz in range(1, ZN):
        exchange(dz).wait_send()

    @pl.when(zh != yl)
    def _():
        exchange(0).wait_send()


def arrange(parts, edge, lower, upper):
    halves = [parts[0, :D], parts[1, :D]]
    edge[...] = jnp.transpose(jnp.concatenate(halves, axis=2), (1, 0, 2))
    lower[:, :HALF] = parts[0, D]
    lower[:, HALF:] = parts[1, D]
    first, second = parts[0, D + 1], parts[1, D + 1]
    upper[...] = jnp.concatenate(
        [first[:, :ROWS], second[:, :ROWS], first[:, ROWS:], second[:, ROWS:]], axis=1
    )


def shards(
    corner_up, edge_top, edge_left, corner_down, edge_bottom, site_weights, proj_upper, proj_lower
):
    vmem = pl.BlockSpec(memory_space=pltpu.VMEM)
    rows2 = YN * ROWS
    size = D * ROWS
    parts = pl.pallas_call(
        kernel,
        out_shape=jax.ShapeDtypeStruct((YN, SLABS, BLK, HALF), BF),
        in_specs=[vmem] * 8,
        out_specs=vmem,
        scratch_shapes=[
            pltpu.VMEM((YN, D, BLK, HALF), BF),
            pltpu.VMEM((D, CHI, HALF), BF),
            pltpu.VMEM((HALF, CHI), BF),
            pltpu.VMEM((D, YN, BLK, CHI), BF),
            pltpu.VMEM((rows2, CHI), BF),
            pltpu.VMEM((rows2, CHI), BF),
            pltpu.VMEM((rows2, CHI), BF),
            pltpu.VMEM((rows2, CHI), BF),
            pltpu.VMEM((YN * BLK, CHI), BF),
            pltpu.VMEM((size, size), BF),
            pltpu.VMEM((YN, size, HALF), BF),
            pltpu.VMEM((D, rows2, HALF), BF),
            pltpu.VMEM((rows2, HALF), BF),
            pltpu.VMEM((4 * HALF + 6 * BLK, HALF), BF),
            pltpu.VMEM((ZN, BLK, HALF), BF),
            pltpu.VMEM((YN, BLK, 4 * HALF), BF),
            pltpu.VMEM((rows2, HALF), BF),
            pltpu.VMEM((SLABS, CHI, HALF), F32),
            pltpu.VMEM((2, 4, YN, SLABS, BLK, HALF), BF),
            pltpu.VMEM((2, 4, YN, SLABS, BLK, HALF), BF),
            pltpu.VMEM((YN, SLABS, BLK, HALF), BF),
            pltpu.SemaphoreType.DMA((COPIES,)),
            pltpu.SemaphoreType.DMA((COPIES,)),
            pltpu.SemaphoreType.DMA((ZN,)),
            pltpu.SemaphoreType.DMA((ZN,)),
            pltpu.SemaphoreType.DMA((8,)),
        ],
        compiler_params=pltpu.CompilerParams(
            collective_id=0, has_side_effects=True, vmem_limit_bytes=56 * 1024 * 1024
        ),
    )(
        proj_upper[0, 0], proj_lower[0, 0], edge_left[0, 0], edge_top[0, 0], edge_bottom[0, 0],
        corner_up[0, 0], corner_down[0, 0], site_weights[0, 0],
    )
    edge, lower, upper = pl.pallas_call(
        arrange,
        out_shape=(
            jax.ShapeDtypeStruct((BLK, D, CHI), BF),
            jax.ShapeDtypeStruct((BLK, CHI), BF),
            jax.ShapeDtypeStruct((BLK, CHI), BF),
        ),
        in_specs=[vmem],
        out_specs=(vmem, vmem, vmem),
    )(parts)
    return upper[None, None], edge[None, None], lower[None, None]


def solution(mesh):
    return jax.shard_map(
        shards,
        mesh=mesh,
        in_specs=(
            P("ux", "uy", "bond", None),
            P("ux", "uy", "bond", None, None),
            P("ux", "uy", "bond", None, None),
            P("ux", "uy", "bond", None),
            P("ux", "uy", "bond", None, None),
            P("ux", "uy", None, None, None, None),
            P("ux", "uy", "bond", None, None),
            P("ux", "uy", "bond", None, None),
        ),
        out_specs=(
            P("ux", "uy", "bond", None),
            P("ux", "uy", "bond", None, None),
            P("ux", "uy", "bond", None),
        ),
        check_vma=False,
    )
```

```python
import jax
import jax.numpy as jnp
from jax import lax
from jax.experimental import pallas as pl
from jax.experimental.pallas import tpu as pltpu
from jax.sharding import PartitionSpec as P

MESH = pl.DeviceIdType.MESH
BF = jnp.bfloat16
F32 = jnp.float32
ZN = 8
YN = 2
D = 4
CHI = 768
BLK = CHI // (ZN * YN)
HALF = CHI // YN
ROWS = D * BLK
SLABS = 6
COPIES = 96


def mul(a, b, ca=1, cb=0):
    return lax.dot_general(a, b, (((ca,), (cb,)), ((), ())), preferred_element_type=F32)


def kernel(
    pu_in, low_in, el_in, et_in, eb_in, cu_in, cd_in, w_in,
    edge_out, lower_out, upper_out,
    pu, low, el, et, eb, w, put, pug, cug, etb, elb, plb, lpb, ebb, cdb, mix, xb, fb, lb, pick, e2, er, ebuf, outp, sbuf, rbuf, fin, fin_edge,
    ssem, rsem, asem, bsem, lsem,
):
    bond = lax.axis_index("bond")
    ux = lax.axis_index("ux")
    uy = lax.axis_index("uy")
    yl = lax.div(bond, ZN)
    z = lax.rem(bond, ZN)
    yo = 1 - yl
    zh = lax.div(z, ZN // 2)
    zq = lax.rem(z, ZN // 2)

    def zmod(k):
        return lax.rem(z + (k + ZN), ZN)

    def at_bond(half, zz, dx=0, dy=0):
        return (lax.rem(ux + (dx + 4), 4), lax.rem(uy + (dy + 4), 4), half * ZN + zz)

    right, left, mate = at_bond(yl, zmod(1)), at_bond(yl, zmod(-1)), at_bond(yo, z)

    my48 = pl.ds(pl.multiple_of(yl * BLK, 16), BLK)
    loads = []
    for i, (src, dst) in enumerate([
        (pu_in, pu), (cu_in, cug.at[pl.ds(pl.multiple_of(z * BLK, 16), BLK), :]), (et_in, et), (low_in, low),
        (el_in, el), (eb_in, eb), (cd_in, cdb.at[my48, :]), (w_in, w),
    ]):
        load = pltpu.make_async_copy(src, dst, lsem.at[i])
        load.start()
        loads.append(load)

    barrier = pltpu.get_barrier_semaphore()
    sources = [
        left, right, mate,
        at_bond(yl, z, dy=-1), at_bond(yo, z, dy=-1), at_bond(yl, z, dx=-1), at_bond(yo, z, dx=-1),
    ]

    def greet(to):
        pl.semaphore_signal(barrier, inc=1, device_id=to, device_id_type=MESH)

    for source in sources:
        greet(source)
    for half in range(YN):
        for q in range(ZN // 2):
            zz = yl * (ZN // 2) + q

            @pl.when(half * ZN + zz != bond)
            def _():
                greet(at_bond(half, zz))

    loads[0].wait()
    turned = jnp.transpose(pu[...], (1, 0, 2))
    put[0] = turned[:, :, :HALF]
    put[1] = turned[:, :, HALF:]
    pl.semaphore_wait(barrier, len(sources) + ZN - jnp.where(zh == yl, 1, 0))

    started = []
    count = [0]

    def rcopy(src, dst, to):
        index = count[0]
        count[0] += 1
        copy = pltpu.make_async_remote_copy(
            src_ref=src, dst_ref=dst, send_sem=ssem.at[index], recv_sem=rsem.at[index],
            device_id=to, device_id_type=MESH,
        )
        copy.start()
        started.append(copy)
        return copy

    def rows_c(half, zz):
        return pl.ds(pl.multiple_of(half * HALF + zz * BLK, 16), BLK)

    def rows_z(zz):
        return pl.ds(pl.multiple_of(zz * BLK, 16), BLK)

    my192 = pl.ds(pl.multiple_of(yl * ROWS, 16), ROWS)

    def pu_at(half, zz):
        return pug.at[:, rows_c(half, zz), :]

    def cu_at(zz, part=None):
        if part is None:
            return cug.at[rows_z(zz), :]
        return cug.at[rows_z(zz), pl.ds(part * HALF, HALF)]

    pr, ql = {}, {}
    pr["own", 1] = rcopy(put.at[yl], pu_at(yl, z), right)
    ql["own", 1] = rcopy(put.at[yl], pu_at(yl, z), left)
    y_pu = rcopy(put.at[yo], pu_at(yl, z), mate)
    loads[1].wait()
    pr["cu", 1] = rcopy(cu_at(z), cu_at(z), right)
    ql["cu", 1] = rcopy(cu_at(z), cu_at(z), left)
    keep = pltpu.make_async_copy(put.at[yl], pu_at(yl, z), lsem.at[8])
    keep.start()
    for load in loads[2:]:
        load.wait()
    etb[:, yl] = jnp.transpose(et[...], (1, 0, 2))
    y_et = rcopy(etb.at[:, yl], etb.at[:, yl], mate)
    plb[my192, :] = jnp.transpose(low[...], (1, 0, 2)).reshape(ROWS, CHI)
    x_same = rcopy(plb.at[my192, :], lpb.at[my192, :], at_bond(yl, z, dy=1))
    x_other = rcopy(plb.at[my192, :], lpb.at[my192, :], at_bond(yo, z, dy=1))
    y_pu.wait_recv()
    pr["oth", 1] = rcopy(pu_at(yo, z), pu_at(yo, z), right)
    ql["oth", 1] = rcopy(pu_at(yo, z), pu_at(yo, z), left)
    elb[my192, :] = jnp.transpose(el[...], (1, 0, 2)).reshape(ROWS, CHI)
    y_el = rcopy(elb.at[my192, :], elb.at[my192, :], mate)
    y_cd = rcopy(cdb.at[my48, :], cdb.at[my48, :], mate)
    ebb[my192, :] = jnp.transpose(eb[...], (1, 0, 2)).reshape(ROWS, CHI)
    y_eb = rcopy(ebb.at[my192, :], ebb.at[my192, :], mate)

    def forward(name, m):
        for flow, sign, to, last in ((pr, -1, right, "own"), (ql, 1, left, "oth")):
            if (name, m) not in flow:
                continue
            flow[name, m].wait_recv()
            zz = zmod(sign * m)
            if name == "cu":
                if m < 4:
                    at = cu_at(zz) if m < 3 else cu_at(zz, 0 if last == "own" else 1)
                    flow[name, m + 1] = rcopy(at, at, to)
            elif m < 3 or (m == 3 and name == last):
                at = pu_at(yl if name == "own" else yo, zz)
                flow[name, m + 1] = rcopy(at, at, to)

    forward("own", 1)
    forward("cu", 1)
    size = D * D * BLK
    rowi = lax.broadcasted_iota(jnp.int32, (size, D ** 3), 0)
    coli = lax.broadcasted_iota(jnp.int32, (size, D ** 3), 1)
    legs = lax.rem(lax.div(rowi, BLK), D) * D + lax.div(rowi, ROWS)
    weights = w[...].reshape(D ** 3, D)
    spread = jnp.zeros((size, D * D), F32)
    for l in range(D):
        one = jnp.where(coli == legs + l * D * D, 1.0, 0.0).astype(BF)
        d_at = lax.broadcasted_iota(jnp.int32, (D, D * D), 0) * D + l
        col = lax.broadcasted_iota(jnp.int32, (D, D * D), 1)
        spread = spread + mul(mul(one, weights).astype(BF), jnp.where(col == d_at, 1.0, 0.0).astype(BF))
    leg = lax.broadcasted_iota(jnp.int32, (D * D, size), 0)
    pos = lax.broadcasted_iota(jnp.int32, (D * D, size), 1)
    expand = jnp.where(leg == lax.div(pos, BLK), 1.0, 0.0).astype(BF)
    full = mul(spread.astype(BF), expand)
    inrow = lax.rem(lax.broadcasted_iota(jnp.int32, (size, 1), 0), BLK)
    incol = lax.rem(lax.broadcasted_iota(jnp.int32, (1, size), 1), BLK)
    mix[...] = jnp.where(inrow == incol, full, 0.0).astype(BF)

    forward("oth", 1)
    forward("cu", 2)
    forward("own", 2)
    forward("oth", 2)
    lane = lax.broadcasted_iota(jnp.int32, (1, HALF), 1)
    second = jnp.where(lane >= ROWS, 1, 0)
    rest = lane - second * ROWS
    target = 3 * 2 * BLK + second * BLK + rest + lax.div(rest, BLK) * (HALF - BLK)
    pick[...] = jnp.where(
        lax.broadcasted_iota(jnp.int32, pick.shape, 0) == target, 1.0, 0.0
    ).astype(BF)

    forward("cu", 3)
    forward("own", 3)
    forward("oth", 3)
    keep.wait()
    y_et.wait_recv()
    forward("cu", 4)
    e2[...] = mul(cug[...], etb[...].reshape(HALF, CHI), 1, 1).astype(BF).reshape(ZN, BLK, HALF)

    def er_at(half, q):
        return er.at[half, :, pl.ds(pl.multiple_of(q * HALF, 128), HALF)]

    slot = yl * (ZN // 2) + zq

    def exchange(dz):
        return pltpu.make_async_remote_copy(
            src_ref=e2.at[zmod(dz)], dst_ref=er_at(yl, zq), send_sem=asem.at[dz], recv_sem=bsem.at[slot],
            device_id=at_bond(zh, zmod(dz)), device_id_type=MESH,
        )

    for dz in (4, 3, 5, 2, 6, 1, 7):
        exchange(dz).start()

    @pl.when(zh == yl)
    def _():
        pltpu.make_async_copy(e2.at[z], er_at(yl, zq), bsem.at[slot]).start()

    @pl.when(zh != yl)
    def _():
        exchange(0).start()

    forward("own", 4)
    forward("oth", 4)
    y_el.wait_recv()
    y_cd.wait_recv()

    def x_step(d, carry):
        x = mul(elb[...], pug[d]).astype(BF)
        base = pl.multiple_of(d * ROWS, 16)
        xb[0, pl.ds(base, ROWS), :] = x[:ROWS]
        xb[1, pl.ds(base, ROWS), :] = x[ROWS:]
        return carry

    lax.fori_loop(0, D, x_step, 0)

    def mix_step(h, carry):
        f = mul(mix[...], xb[h]).astype(BF)
        for r in range(D):
            fb[r, pl.ds(pl.multiple_of(h * ROWS, 16), ROWS), :] = f[r * ROWS:(r + 1) * ROWS]
        return carry

    lax.fori_loop(0, YN, mix_step, 0)
    x_same.wait_recv()
    x_other.wait_recv()

    def edge_step(r, carry):
        outp[r] = mul(lpb[...], fb[r], 0, 0)
        return carry

    def own(j0, n, h, zz):
        return outp[j0:j0 + n, pl.ds(pl.multiple_of(h * HALF + zz * BLK, 16), BLK), :]

    flows = {}

    def rs_first(j0, n):
        zz = zmod(4)
        for side, h, to in ((0, 0, right), (1, 1, left)):
            sbuf[side, 0, h, j0:j0 + n] = own(j0, n, h, zz).astype(BF)
            flows[j0, side, 1] = rcopy(
                sbuf.at[side, 0, h, pl.ds(j0, n)], rbuf.at[side, 0, h, pl.ds(j0, n)], to
            )

    def rs_next(j0, n, t):
        for side, sign, to in ((0, 1, right), (1, -1, left)):
            flows[j0, side, t - 1].wait_recv()
            zz = zmod(sign * (5 - t))
            for h in range(YN):
                value = own(j0, n, h, zz)
                if t > 2 or h == side:
                    value = value + rbuf[side, t - 2, h, j0:j0 + n].astype(F32)
                sbuf[side, t - 1, h, j0:j0 + n] = value.astype(BF)
            flows[j0, side, t] = rcopy(
                sbuf.at[side, t - 1, :, pl.ds(j0, n)], rbuf.at[side, t - 1, :, pl.ds(j0, n)], to
            )

    def rs_sum(j0, n, h):
        value = own(j0, n, h, z)
        for side in range(2):
            value = value + rbuf[side, 3, h, j0:j0 + n].astype(F32)
        return value.astype(BF)

    def rs_end(j0):
        for side in range(2):
            flows[j0, side, 4].wait_recv()

    def deliver(src, dst):
        return [rcopy(src.at[yl], dst, at_bond(yl, z, dx=1)), rcopy(src.at[yo], dst, at_bond(yo, z, dx=1))]

    mylanes = pl.ds(pl.multiple_of(yl * HALF, 128), HALF)
    waves = [(0, 2), (2, 2), (4, 1), (5, 1)]
    lax.fori_loop(0, 2, edge_step, 0)
    rs_first(0, 2)
    lax.fori_loop(2, 4, edge_step, 0)
    rs_first(2, 2)

    def low_step(d, carry):
        part = mul(cdb[...], pug[d]).astype(BF)
        lb[pl.ds(pl.multiple_of(d * BLK, 16), BLK), :] = part[:BLK]
        lb[pl.ds(pl.multiple_of(ROWS + d * BLK, 16), BLK), :] = part[BLK:]
        return carry

    lax.fori_loop(0, D, low_step, 0)
    y_eb.wait_recv()
    outp[4] = mul(ebb[...], lb[...], 0, 0)
    rs_first(4, 1)
    rs_next(0, 2, 2)
    for half in range(YN):
        for q in range(ZN // 2):
            pltpu.make_async_copy(e2.at[0], er_at(half, q), bsem.at[half * (ZN // 2) + q]).wait()

    def pick_step(k, carry):
        shift = pl.multiple_of((3 - k) * 2 * BLK, 16)
        part = mul(er[...].reshape(YN * BLK, 4 * HALF), pick[pl.ds(shift, 4 * HALF), :]).astype(BF)
        ebuf[pl.ds(pl.multiple_of(k * BLK, 16), BLK), :] = part[:BLK]
        ebuf[pl.ds(pl.multiple_of(ROWS + k * BLK, 16), BLK), :] = part[BLK:]
        return carry

    lax.fori_loop(0, D, pick_step, 0)
    outp[5] = mul(lpb[...], ebuf[...], 0, 0)
    rs_first(5, 1)
    for j0, n in waves[1:]:
        rs_next(j0, n, 2)
    for t in (3, 4):
        for j0, n in waves:
            rs_next(j0, n, t)
    before = list(started)
    rs_end(0)
    rs_end(2)
    for h in range(YN):
        fin_edge[h] = jnp.transpose(rs_sum(0, D, h), (1, 0, 2))
    outs = deliver(fin_edge, edge_out.at[:, :, mylanes])
    rs_end(4)
    for h in range(YN):
        fin[h, 0] = rs_sum(D, 1, h)[0]
    outs += deliver(fin.at[:, 0], lower_out.at[:, mylanes])
    rs_end(5)
    for h in range(YN):
        fin[h, 1] = rs_sum(D + 1, 1, h)[0]
    outs += deliver(fin.at[:, 1], upper_out.at[yl])
    for copy in before:
        copy.wait_send()
    for dz in range(1, ZN):
        exchange(dz).wait_send()

    @pl.when(zh != yl)
    def _():
        exchange(0).wait_send()

    for copy in outs:
        copy.wait_recv()
    for copy in outs:
        copy.wait_send()


def settle(edge_in, lower_in, upper_in, edge_out, lower_out, upper_out, edge, lower, parts, upper, sems):
    def move(i, src, dst):
        copy = pltpu.make_async_copy(src, dst, sems.at[i])
        copy.start()
        return copy

    arrived = [move(0, edge_in, edge), move(1, upper_in, parts), move(2, lower_in, lower)]
    arrived[0].wait()
    sent = [move(3, edge, edge_out)]
    arrived[1].wait()
    first, second = parts[0], parts[1]
    upper[...] = jnp.concatenate(
        [first[:, :ROWS], second[:, :ROWS], first[:, ROWS:], second[:, ROWS:]], axis=1
    )
    sent.append(move(4, upper, upper_out))
    arrived[2].wait()
    sent.append(move(5, lower, lower_out))
    for copy in sent:
        copy.wait()


def shards(
    corner_up, edge_top, edge_left, corner_down, edge_bottom, site_weights, proj_upper, proj_lower
):
    rows2 = YN * ROWS
    size = D * ROWS
    hbm = pl.BlockSpec(memory_space=pl.ANY)
    edge, lower, upper = pl.pallas_call(
        kernel,
        out_shape=(
            jax.ShapeDtypeStruct((BLK, D, CHI), BF),
            jax.ShapeDtypeStruct((BLK, CHI), BF),
            jax.ShapeDtypeStruct((YN, BLK, HALF), BF),
        ),
        in_specs=[hbm] * 8,
        out_specs=(hbm,) * 3,
        scratch_shapes=[
            *[pltpu.VMEM((BLK, D, CHI), BF)] * 5,
            pltpu.VMEM((D, D, D, D), BF),
            pltpu.VMEM((YN, D, BLK, HALF), BF),
            pltpu.VMEM((D, CHI, HALF), BF),
            pltpu.VMEM((HALF, CHI), BF),
            pltpu.VMEM((D, YN, BLK, CHI), BF),
            pltpu.VMEM((rows2, CHI), BF),
            pltpu.VMEM((rows2, CHI), BF),
            pltpu.VMEM((rows2, CHI), BF),
            pltpu.VMEM((rows2, CHI), BF),
            pltpu.VMEM((YN * BLK, CHI), BF),
            pltpu.VMEM((size, size), BF),
            pltpu.VMEM((YN, size, HALF), BF),
            pltpu.VMEM((D, rows2, HALF), BF),
            pltpu.VMEM((rows2, HALF), BF),
            pltpu.VMEM((4 * HALF + 6 * BLK, HALF), BF),
            pltpu.VMEM((ZN, BLK, HALF), BF),
            pltpu.VMEM((YN, BLK, 4 * HALF), BF),
            pltpu.VMEM((rows2, HALF), BF),
            pltpu.VMEM((SLABS, CHI, HALF), F32),
            pltpu.VMEM((2, 4, YN, SLABS, BLK, HALF), BF),
            pltpu.VMEM((2, 4, YN, SLABS, BLK, HALF), BF),
            pltpu.VMEM((YN, 2, BLK, HALF), BF),
            pltpu.VMEM((YN, BLK, D, HALF), BF),
            pltpu.SemaphoreType.DMA((COPIES,)),
            pltpu.SemaphoreType.DMA((COPIES,)),
            pltpu.SemaphoreType.DMA((ZN,)),
            pltpu.SemaphoreType.DMA((ZN,)),
            pltpu.SemaphoreType.DMA((9,)),
        ],
        compiler_params=pltpu.CompilerParams(
            collective_id=0, has_side_effects=True, vmem_limit_bytes=56 * 1024 * 1024
        ),
    )(
        proj_upper[0, 0], proj_lower[0, 0], edge_left[0, 0], edge_top[0, 0], edge_bottom[0, 0],
        corner_up[0, 0], corner_down[0, 0], site_weights[0, 0],
    )
    edge, lower, upper = pl.pallas_call(
        settle,
        out_shape=(
            jax.ShapeDtypeStruct((BLK, D, CHI), BF),
            jax.ShapeDtypeStruct((BLK, CHI), BF),
            jax.ShapeDtypeStruct((BLK, CHI), BF),
        ),
        in_specs=[hbm] * 3,
        out_specs=(hbm,) * 3,
        scratch_shapes=[
            pltpu.VMEM((BLK, D, CHI), BF),
            pltpu.VMEM((BLK, CHI), BF),
            pltpu.VMEM((YN, BLK, HALF), BF),
            pltpu.VMEM((BLK, CHI), BF),
            pltpu.SemaphoreType.DMA((6,)),
        ],
    )(edge, lower, upper)
    return upper[None, None], edge[None, None], lower[None, None]


def solution(mesh):
    return jax.shard_map(
        shards,
        mesh=mesh,
        in_specs=(
            P("ux", "uy", "bond", None),
            P("ux", "uy", "bond", None, None),
            P("ux", "uy", "bond", None, None),
            P("ux", "uy", "bond", None),
            P("ux", "uy", "bond", None, None),
            P("ux", "uy", None, None, None, None),
            P("ux", "uy", "bond", None, None),
            P("ux", "uy", "bond", None, None),
        ),
        out_specs=(
            P("ux", "uy", "bond", None),
            P("ux", "uy", "bond", None, None),
            P("ux", "uy", "bond", None),
        ),
        check_vma=False,
    )
```

```python
import jax
import jax.numpy as jnp
from jax import lax
from jax.experimental import pallas as pl
from jax.experimental.pallas import tpu as pltpu
from jax.sharding import PartitionSpec as P

MESH = pl.DeviceIdType.MESH
BF = jnp.bfloat16
F32 = jnp.float32
ZN = 8
YN = 2
D = 4
CHI = 768
BLK = CHI // (ZN * YN)
HALF = CHI // YN
ROWS = D * BLK
LANE = 128
CUTS = HALF // LANE
TILE = 16
LOWER = CUTS * D
UPPER = LOWER + CUTS
UNITS = UPPER + CUTS
COPIES = 128


def mul(a, b, ca=1, cb=0):
    return lax.dot_general(a, b, (((ca,), (cb,)), ((), ())), preferred_element_type=F32)


def kernel(
    pu_in, low_in, el_in, et_in, eb_in, cu_in, cd_in, w_in,
    edge_out, lower_out, upper_out,
    pu, low, el, et, eb, w, put, pug, cug, etb, elb, plb, lpb, ebb, cdb, mix, xb, fb, lpt, lb, pick, e2, er, ebuf, outp, sbuf, rbuf, fin, fin_edge,
    ssem, rsem, asem, bsem, lsem,
):
    bond = lax.axis_index("bond")
    ux = lax.axis_index("ux")
    uy = lax.axis_index("uy")
    yl = lax.div(bond, ZN)
    z = lax.rem(bond, ZN)
    yo = 1 - yl
    zh = lax.div(z, ZN // 2)
    zq = lax.rem(z, ZN // 2)

    def zmod(k):
        return lax.rem(z + (k + ZN), ZN)

    def at_bond(half, zz, dx=0, dy=0):
        return (lax.rem(ux + (dx + 4), 4), lax.rem(uy + (dy + 4), 4), half * ZN + zz)

    right, left, mate = at_bond(yl, zmod(1)), at_bond(yl, zmod(-1)), at_bond(yo, z)

    my48 = pl.ds(pl.multiple_of(yl * BLK, 16), BLK)
    loads = []
    for i, (src, dst) in enumerate([
        (pu_in, pu), (cu_in, cug.at[pl.ds(pl.multiple_of(z * BLK, 16), BLK), :]), (et_in, et), (low_in, low),
        (el_in, el), (eb_in, eb), (cd_in, cdb.at[my48, :]), (w_in, w),
    ]):
        load = pltpu.make_async_copy(src, dst, lsem.at[i])
        load.start()
        loads.append(load)

    barrier = pltpu.get_barrier_semaphore()
    sources = [
        left, right, mate,
        at_bond(yl, z, dy=-1), at_bond(yo, z, dy=-1), at_bond(yl, z, dx=-1), at_bond(yo, z, dx=-1),
    ]

    def greet(to):
        pl.semaphore_signal(barrier, inc=1, device_id=to, device_id_type=MESH)

    for source in sources:
        greet(source)
    for half in range(YN):
        for q in range(ZN // 2):
            zz = yl * (ZN // 2) + q

            @pl.when(half * ZN + zz != bond)
            def _():
                greet(at_bond(half, zz))

    loads[0].wait()
    turned = jnp.transpose(pu[...], (1, 0, 2))
    put[0] = turned[:, :, :HALF]
    put[1] = turned[:, :, HALF:]
    pl.semaphore_wait(barrier, len(sources) + ZN - jnp.where(zh == yl, 1, 0))

    started = []
    count = [0]

    def rcopy(src, dst, to):
        index = count[0]
        count[0] += 1
        copy = pltpu.make_async_remote_copy(
            src_ref=src, dst_ref=dst, send_sem=ssem.at[index], recv_sem=rsem.at[index],
            device_id=to, device_id_type=MESH,
        )
        copy.start()
        started.append(copy)
        return copy

    def rows_c(half, zz):
        return pl.ds(pl.multiple_of(half * HALF + zz * BLK, 16), BLK)

    def rows_z(zz):
        return pl.ds(pl.multiple_of(zz * BLK, 16), BLK)

    my192 = pl.ds(pl.multiple_of(yl * ROWS, 16), ROWS)

    def pu_at(half, zz):
        return pug.at[:, rows_c(half, zz), :]

    def cu_at(zz, part=None):
        if part is None:
            return cug.at[rows_z(zz), :]
        return cug.at[rows_z(zz), pl.ds(part * HALF, HALF)]

    pr, ql = {}, {}
    pr["own", 1] = rcopy(put.at[yl], pu_at(yl, z), right)
    ql["own", 1] = rcopy(put.at[yl], pu_at(yl, z), left)
    y_pu = rcopy(put.at[yo], pu_at(yl, z), mate)
    loads[1].wait()
    pr["cu", 1] = rcopy(cu_at(z), cu_at(z), right)
    ql["cu", 1] = rcopy(cu_at(z), cu_at(z), left)
    keep = pltpu.make_async_copy(put.at[yl], pu_at(yl, z), lsem.at[8])
    keep.start()
    for load in loads[2:]:
        load.wait()
    etb[:, yl] = jnp.transpose(et[...], (1, 0, 2))
    y_et = rcopy(etb.at[:, yl], etb.at[:, yl], mate)
    plb[my192, :] = jnp.transpose(low[...], (1, 0, 2)).reshape(ROWS, CHI)
    x_same = rcopy(plb.at[my192, :], lpb.at[my192, :], at_bond(yl, z, dy=1))
    x_other = rcopy(plb.at[my192, :], lpb.at[my192, :], at_bond(yo, z, dy=1))
    y_pu.wait_recv()
    pr["oth", 1] = rcopy(pu_at(yo, z), pu_at(yo, z), right)
    ql["oth", 1] = rcopy(pu_at(yo, z), pu_at(yo, z), left)
    elb[my192, :] = jnp.transpose(el[...], (1, 0, 2)).reshape(ROWS, CHI)
    y_el = rcopy(elb.at[my192, :], elb.at[my192, :], mate)
    y_cd = rcopy(cdb.at[my48, :], cdb.at[my48, :], mate)
    ebb[my192, :] = jnp.transpose(eb[...], (1, 0, 2)).reshape(ROWS, CHI)
    y_eb = rcopy(ebb.at[my192, :], ebb.at[my192, :], mate)

    def forward(name, m):
        for flow, sign, to, last in ((pr, -1, right, "own"), (ql, 1, left, "oth")):
            if (name, m) not in flow:
                continue
            flow[name, m].wait_recv()
            zz = zmod(sign * m)
            if name == "cu":
                if m < 4:
                    at = cu_at(zz) if m < 3 else cu_at(zz, 0 if last == "own" else 1)
                    flow[name, m + 1] = rcopy(at, at, to)
            elif m < 3 or (m == 3 and name == last):
                at = pu_at(yl if name == "own" else yo, zz)
                flow[name, m + 1] = rcopy(at, at, to)

    forward("own", 1)
    forward("cu", 1)
    size = D * D * TILE
    rowi = lax.broadcasted_iota(jnp.int32, (size, D ** 3), 0)
    coli = lax.broadcasted_iota(jnp.int32, (size, D ** 3), 1)
    legs = lax.rem(lax.div(rowi, TILE), D) * D + lax.div(rowi, D * TILE)
    weights = w[...].reshape(D ** 3, D)
    spread = jnp.zeros((size, D * D), F32)
    for l in range(D):
        one = jnp.where(coli == legs + l * D * D, 1.0, 0.0).astype(BF)
        d_at = lax.broadcasted_iota(jnp.int32, (D, D * D), 0) * D + l
        col = lax.broadcasted_iota(jnp.int32, (D, D * D), 1)
        spread = spread + mul(mul(one, weights).astype(BF), jnp.where(col == d_at, 1.0, 0.0).astype(BF))
    leg = lax.broadcasted_iota(jnp.int32, (D * D, size), 0)
    pos = lax.broadcasted_iota(jnp.int32, (D * D, size), 1)
    expand = jnp.where(leg == lax.div(pos, TILE), 1.0, 0.0).astype(BF)
    full = mul(spread.astype(BF), expand)
    inrow = lax.rem(lax.broadcasted_iota(jnp.int32, (size, 1), 0), TILE)
    incol = lax.rem(lax.broadcasted_iota(jnp.int32, (1, size), 1), TILE)
    mix[...] = jnp.where(inrow == incol, full, 0.0).astype(BF)

    forward("oth", 1)
    forward("cu", 2)
    forward("own", 2)
    forward("oth", 2)
    x_same.wait_recv()
    x_other.wait_recv()
    lpt[...] = lpb[...].T
    lane = lax.broadcasted_iota(jnp.int32, (1, HALF), 1)
    second = jnp.where(lane >= ROWS, 1, 0)
    rest = lane - second * ROWS
    target = 3 * 2 * BLK + second * BLK + rest + lax.div(rest, BLK) * (HALF - BLK)
    pick[...] = jnp.where(
        lax.broadcasted_iota(jnp.int32, pick.shape, 0) == target, 1.0, 0.0
    ).astype(BF)

    forward("cu", 3)
    forward("own", 3)
    forward("oth", 3)
    keep.wait()
    y_et.wait_recv()
    forward("cu", 4)
    e2[...] = mul(cug[...], etb[...].reshape(HALF, CHI), 1, 1).astype(BF).reshape(ZN, BLK, HALF)

    def er_at(half, q):
        return er.at[half, :, pl.ds(pl.multiple_of(q * HALF, 128), HALF)]

    slot = yl * (ZN // 2) + zq

    def exchange(dz):
        return pltpu.make_async_remote_copy(
            src_ref=e2.at[zmod(dz)], dst_ref=er_at(yl, zq), send_sem=asem.at[dz], recv_sem=bsem.at[slot],
            device_id=at_bond(zh, zmod(dz)), device_id_type=MESH,
        )

    for dz in (4, 3, 5, 2, 6, 1, 7):
        exchange(dz).start()

    @pl.when(zh == yl)
    def _():
        pltpu.make_async_copy(e2.at[z], er_at(yl, zq), bsem.at[slot]).start()

    @pl.when(zh != yl)
    def _():
        exchange(0).start()

    forward("own", 4)
    forward("oth", 4)
    y_el.wait_recv()
    y_cd.wait_recv()

    for d in range(D):
        x = mul(elb[...], pug[d]).astype(BF)
        for h in range(YN):
            for l in range(D):
                for c in range(BLK // TILE):
                    row = h * ROWS + l * BLK + c * TILE
                    to = (d * D + l) * TILE
                    xb[h, c, to:to + TILE, :] = x[row:row + TILE]
    for h in range(YN):
        for c in range(BLK // TILE):
            f = mul(mix[...], xb[h, c]).astype(BF)
            for i in range(CUTS):
                for r in range(D):
                    for u in range(D):
                        row = h * ROWS + u * BLK + c * TILE
                        part = f[(r * D + u) * TILE:(r * D + u + 1) * TILE, i * LANE:(i + 1) * LANE]
                        fb[i, row:row + TILE, r * LANE:(r + 1) * LANE] = part

    def edge_step(i):
        part = mul(lpt[...], fb[i])
        for r in range(D):
            outp[i * D + r] = part[:, r * LANE:(r + 1) * LANE]

    def own(j0, n, h, zz):
        return outp[j0:j0 + n, pl.ds(pl.multiple_of(h * HALF + zz * BLK, 16), BLK), :]

    flows = {}

    def rs_first(j0, n):
        zz = zmod(4)
        for side, h, to in ((0, 0, right), (1, 1, left)):
            sbuf[side, 0, h, j0:j0 + n] = own(j0, n, h, zz).astype(BF)
            flows[j0, side, 1] = rcopy(
                sbuf.at[side, 0, h, pl.ds(j0, n)], rbuf.at[side, 0, h, pl.ds(j0, n)], to
            )

    def rs_next(j0, n, t):
        for side, sign, to in ((0, 1, right), (1, -1, left)):
            flows[j0, side, t - 1].wait_recv()
            zz = zmod(sign * (5 - t))
            for h in range(YN):
                value = own(j0, n, h, zz)
                if t > 2 or h == side:
                    value = value + rbuf[side, t - 2, h, j0:j0 + n].astype(F32)
                sbuf[side, t - 1, h, j0:j0 + n] = value.astype(BF)
            flows[j0, side, t] = rcopy(
                sbuf.at[side, t - 1, :, pl.ds(j0, n)], rbuf.at[side, t - 1, :, pl.ds(j0, n)], to
            )

    def rs_sum(j0, n, h):
        value = own(j0, n, h, z)
        for side in range(2):
            value = value + rbuf[side, 3, h, j0:j0 + n].astype(F32)
        return value.astype(BF)

    def rs_end(j0):
        for side in range(2):
            flows[j0, side, 4].wait_recv()

    def deliver(src, dst):
        return [rcopy(src.at[yl], dst, at_bond(yl, z, dx=1)), rcopy(src.at[yo], dst, at_bond(yo, z, dx=1))]

    waves = [(i * D, D) for i in range(CUTS)] + [(LOWER, CUTS), (UPPER, CUTS)]
    for i in range(CUTS):
        edge_step(i)
        rs_first(i * D, D)

    def low_step(d, carry):
        part = mul(cdb[...], pug[d]).astype(BF)
        lb[pl.ds(pl.multiple_of(d * BLK, 16), BLK), :] = part[:BLK]
        lb[pl.ds(pl.multiple_of(ROWS + d * BLK, 16), BLK), :] = part[BLK:]
        return carry

    lax.fori_loop(0, D, low_step, 0)
    y_eb.wait_recv()
    part = mul(ebb[...], lb[...], 0, 0)
    for i in range(CUTS):
        outp[LOWER + i] = part[:, i * LANE:(i + 1) * LANE]
    rs_first(LOWER, CUTS)
    rs_next(0, D, 2)
    for half in range(YN):
        for q in range(ZN // 2):
            pltpu.make_async_copy(e2.at[0], er_at(half, q), bsem.at[half * (ZN // 2) + q]).wait()

    def pick_step(k, carry):
        shift = pl.multiple_of((3 - k) * 2 * BLK, 16)
        part = mul(er[...].reshape(YN * BLK, 4 * HALF), pick[pl.ds(shift, 4 * HALF), :]).astype(BF)
        ebuf[pl.ds(pl.multiple_of(k * BLK, 16), BLK), :] = part[:BLK]
        ebuf[pl.ds(pl.multiple_of(ROWS + k * BLK, 16), BLK), :] = part[BLK:]
        return carry

    lax.fori_loop(0, D, pick_step, 0)
    part = mul(lpt[...], ebuf[...])
    for i in range(CUTS):
        outp[UPPER + i] = part[:, i * LANE:(i + 1) * LANE]
    rs_first(UPPER, CUTS)
    for j0, n in waves[1:]:
        rs_next(j0, n, 2)
    for t in (3, 4):
        for j0, n in waves:
            rs_next(j0, n, t)
    before = list(started)
    outs = []
    for i in range(CUTS):
        rs_end(i * D)
        for h in range(YN):
            fin_edge[i, h] = jnp.transpose(rs_sum(i * D, D, h), (1, 0, 2))
        lanes = pl.ds(pl.multiple_of(yl * HALF + i * LANE, LANE), LANE)
        outs += deliver(fin_edge.at[i], edge_out.at[:, :, lanes])
    for j, (j0, dst) in enumerate((
        (LOWER, lower_out.at[:, pl.ds(pl.multiple_of(yl * HALF, LANE), HALF)]), (UPPER, upper_out.at[yl])
    )):
        rs_end(j0)
        for h in range(YN):
            total = rs_sum(j0, CUTS, h)
            for i in range(CUTS):
                fin[j, h, :, i * LANE:(i + 1) * LANE] = total[i]
        outs += deliver(fin.at[j], dst)
    for copy in before:
        copy.wait_send()
    for dz in range(1, ZN):
        exchange(dz).wait_send()

    @pl.when(zh != yl)
    def _():
        exchange(0).wait_send()

    for copy in outs:
        copy.wait_recv()
    for copy in outs:
        copy.wait_send()


def settle(edge_in, lower_in, upper_in, edge_out, lower_out, upper_out, edge, lower, parts, upper, sems):
    def move(i, src, dst):
        copy = pltpu.make_async_copy(src, dst, sems.at[i])
        copy.start()
        return copy

    arrived = [move(0, edge_in, edge), move(1, upper_in, parts), move(2, lower_in, lower)]
    arrived[0].wait()
    sent = [move(3, edge, edge_out)]
    arrived[1].wait()
    first, second = parts[0], parts[1]
    upper[...] = jnp.concatenate(
        [first[:, :ROWS], second[:, :ROWS], first[:, ROWS:], second[:, ROWS:]], axis=1
    )
    sent.append(move(4, upper, upper_out))
    arrived[2].wait()
    sent.append(move(5, lower, lower_out))
    for copy in sent:
        copy.wait()


def shards(
    corner_up, edge_top, edge_left, corner_down, edge_bottom, site_weights, proj_upper, proj_lower
):
    rows2 = YN * ROWS
    size = D * D * TILE
    hbm = pl.BlockSpec(memory_space=pl.ANY)
    edge, lower, upper = pl.pallas_call(
        kernel,
        out_shape=(
            jax.ShapeDtypeStruct((BLK, D, CHI), BF),
            jax.ShapeDtypeStruct((BLK, CHI), BF),
            jax.ShapeDtypeStruct((YN, BLK, HALF), BF),
        ),
        in_specs=[hbm] * 8,
        out_specs=(hbm,) * 3,
        scratch_shapes=[
            *[pltpu.VMEM((BLK, D, CHI), BF)] * 5,
            pltpu.VMEM((D, D, D, D), BF),
            pltpu.VMEM((YN, D, BLK, HALF), BF),
            pltpu.VMEM((D, CHI, HALF), BF),
            pltpu.VMEM((HALF, CHI), BF),
            pltpu.VMEM((D, YN, BLK, CHI), BF),
            pltpu.VMEM((rows2, CHI), BF),
            pltpu.VMEM((rows2, CHI), BF),
            pltpu.VMEM((rows2, CHI), BF),
            pltpu.VMEM((rows2, CHI), BF),
            pltpu.VMEM((YN * BLK, CHI), BF),
            pltpu.VMEM((size, size), BF),
            pltpu.VMEM((YN, BLK // TILE, size, HALF), BF),
            pltpu.VMEM((CUTS, rows2, D * LANE), BF),
            pltpu.VMEM((CHI, rows2), BF),
            pltpu.VMEM((rows2, HALF), BF),
            pltpu.VMEM((4 * HALF + 6 * BLK, HALF), BF),
            pltpu.VMEM((ZN, BLK, HALF), BF),
            pltpu.VMEM((YN, BLK, 4 * HALF), BF),
            pltpu.VMEM((rows2, HALF), BF),
            pltpu.VMEM((UNITS, CHI, LANE), F32),
            pltpu.VMEM((2, 4, YN, UNITS, BLK, LANE), BF),
            pltpu.VMEM((2, 4, YN, UNITS, BLK, LANE), BF),
            pltpu.VMEM((2, YN, BLK, HALF), BF),
            pltpu.VMEM((CUTS, YN, BLK, D, LANE), BF),
            pltpu.SemaphoreType.DMA((COPIES,)),
            pltpu.SemaphoreType.DMA((COPIES,)),
            pltpu.SemaphoreType.DMA((ZN,)),
            pltpu.SemaphoreType.DMA((ZN,)),
            pltpu.SemaphoreType.DMA((9,)),
        ],
        compiler_params=pltpu.CompilerParams(
            collective_id=0, has_side_effects=True, vmem_limit_bytes=56 * 1024 * 1024
        ),
    )(
        proj_upper[0, 0], proj_lower[0, 0], edge_left[0, 0], edge_top[0, 0], edge_bottom[0, 0],
        corner_up[0, 0], corner_down[0, 0], site_weights[0, 0],
    )
    edge, lower, upper = pl.pallas_call(
        settle,
        out_shape=(
            jax.ShapeDtypeStruct((BLK, D, CHI), BF),
            jax.ShapeDtypeStruct((BLK, CHI), BF),
            jax.ShapeDtypeStruct((BLK, CHI), BF),
        ),
        in_specs=[hbm] * 3,
        out_specs=(hbm,) * 3,
        scratch_shapes=[
            pltpu.VMEM((BLK, D, CHI), BF),
            pltpu.VMEM((BLK, CHI), BF),
            pltpu.VMEM((YN, BLK, HALF), BF),
            pltpu.VMEM((BLK, CHI), BF),
            pltpu.SemaphoreType.DMA((6,)),
        ],
    )(edge, lower, upper)
    return upper[None, None], edge[None, None], lower[None, None]


def solution(mesh):
    return jax.shard_map(
        shards,
        mesh=mesh,
        in_specs=(
            P("ux", "uy", "bond", None),
            P("ux", "uy", "bond", None, None),
            P("ux", "uy", "bond", None, None),
            P("ux", "uy", "bond", None),
            P("ux", "uy", "bond", None, None),
            P("ux", "uy", None, None, None, None),
            P("ux", "uy", "bond", None, None),
            P("ux", "uy", "bond", None, None),
        ),
        out_specs=(
            P("ux", "uy", "bond", None),
            P("ux", "uy", "bond", None, None),
            P("ux", "uy", "bond", None),
        ),
        check_vma=False,
    )
```

```python
import jax
import jax.numpy as jnp
from jax import lax
from jax.experimental import pallas as pl
from jax.experimental.pallas import tpu as pltpu
from jax.sharding import PartitionSpec as P

MESH = pl.DeviceIdType.MESH
BF = jnp.bfloat16
F32 = jnp.float32
ZN = 8
YN = 2
D = 4
CHI = 768
BLK = CHI // (ZN * YN)
HALF = CHI // YN
ROWS = D * BLK
LANE = 128
CUTS = HALF // LANE
TILE = 16
LOWER = CUTS * D
UPPER = LOWER + CUTS
UNITS = UPPER + CUTS
COPIES = 79
SENDS = 24


def mul(a, b, ca=1, cb=0):
    return lax.dot_general(a, b, (((ca,), (cb,)), ((), ())), preferred_element_type=F32)


def kernel(
    pu_in, low_in, el_in, et_in, eb_in, cu_in, cd_in, w_in,
    edge_out, lower_out, upper_out,
    pu, low, el, et, eb, w, put, pug, cug, etb, elb, plb, lpb, ebb, cdb, mix, xb, fb, lpt, lb, pick, e2, er, ebuf, outp, sbuf, rbuf, fin, fin_edge,
    ssem, rsem, asem, bsem, lsem,
):
    bond = lax.axis_index("bond")
    ux = lax.axis_index("ux")
    uy = lax.axis_index("uy")
    yl = lax.div(bond, ZN)
    z = lax.rem(bond, ZN)
    yo = 1 - yl
    zh = lax.div(z, ZN // 2)
    zq = lax.rem(z, ZN // 2)

    def zmod(k):
        return lax.rem(z + (k + ZN), ZN)

    def at_bond(half, zz, dx=0, dy=0):
        return (lax.rem(ux + (dx + 4), 4), lax.rem(uy + (dy + 4), 4), half * ZN + zz)

    right, left, mate = at_bond(yl, zmod(1)), at_bond(yl, zmod(-1)), at_bond(yo, z)

    my48 = pl.ds(pl.multiple_of(yl * BLK, 16), BLK)
    loads = []
    for i, (src, dst) in enumerate([
        (pu_in, pu), (cu_in, cug.at[pl.ds(pl.multiple_of(z * BLK, 16), BLK), :]), (et_in, et), (low_in, low),
        (el_in, el), (eb_in, eb), (cd_in, cdb.at[my48, :]), (w_in, w),
    ]):
        load = pltpu.make_async_copy(src, dst, lsem.at[i])
        load.start()
        loads.append(load)

    barrier = pltpu.get_barrier_semaphore()
    sources = [
        left, right, mate,
        at_bond(yl, z, dy=-1), at_bond(yo, z, dy=-1), at_bond(yl, z, dx=-1), at_bond(yo, z, dx=-1),
    ]

    def greet(to):
        pl.semaphore_signal(barrier, inc=1, device_id=to, device_id_type=MESH)

    for source in sources:
        greet(source)
    for half in range(YN):
        for q in range(ZN // 2):
            zz = yl * (ZN // 2) + q

            @pl.when(half * ZN + zz != bond)
            def _():
                greet(at_bond(half, zz))

    loads[0].wait()
    turned = jnp.transpose(pu[...], (1, 0, 2))
    put[0] = turned[:, :, :HALF]
    put[1] = turned[:, :, HALF:]
    pl.semaphore_wait(barrier, len(sources) + ZN - jnp.where(zh == yl, 1, 0))

    started = []

    def rcopy(src, dst, to):
        index = len(started)
        if index >= SENDS:
            started[index - SENDS].wait_send()
        copy = pltpu.make_async_remote_copy(
            src_ref=src, dst_ref=dst, send_sem=ssem.at[index % SENDS], recv_sem=rsem.at[index],
            device_id=to, device_id_type=MESH,
        )
        copy.start()
        started.append(copy)
        return copy

    def rows_c(half, zz):
        return pl.ds(pl.multiple_of(half * HALF + zz * BLK, 16), BLK)

    def rows_z(zz):
        return pl.ds(pl.multiple_of(zz * BLK, 16), BLK)

    my192 = pl.ds(pl.multiple_of(yl * ROWS, 16), ROWS)

    def pu_at(half, zz):
        return pug.at[:, rows_c(half, zz), :]

    def cu_at(zz, part=None):
        if part is None:
            return cug.at[rows_z(zz), :]
        return cug.at[rows_z(zz), pl.ds(part * HALF, HALF)]

    pr, ql = {}, {}
    pr["own", 1] = rcopy(put.at[yl], pu_at(yl, z), right)
    ql["own", 1] = rcopy(put.at[yl], pu_at(yl, z), left)
    y_pu = rcopy(put.at[yo], pu_at(yl, z), mate)
    loads[1].wait()
    pr["cu", 1] = rcopy(cu_at(z), cu_at(z), right)
    ql["cu", 1] = rcopy(cu_at(z), cu_at(z), left)
    keep = pltpu.make_async_copy(put.at[yl], pu_at(yl, z), lsem.at[8])
    keep.start()
    for load in loads[2:]:
        load.wait()
    etb[:, yl] = jnp.transpose(et[...], (1, 0, 2))
    y_et = rcopy(etb.at[:, yl], etb.at[:, yl], mate)
    plb[my192, :] = jnp.transpose(low[...], (1, 0, 2)).reshape(ROWS, CHI)
    x_same = rcopy(plb.at[my192, :], lpb.at[my192, :], at_bond(yl, z, dy=1))
    x_other = rcopy(plb.at[my192, :], lpb.at[my192, :], at_bond(yo, z, dy=1))
    y_pu.wait_recv()
    pr["oth", 1] = rcopy(pu_at(yo, z), pu_at(yo, z), right)
    ql["oth", 1] = rcopy(pu_at(yo, z), pu_at(yo, z), left)
    elb[my192, :] = jnp.transpose(el[...], (1, 0, 2)).reshape(ROWS, CHI)
    y_el = rcopy(elb.at[my192, :], elb.at[my192, :], mate)
    y_cd = rcopy(cdb.at[my48, :], cdb.at[my48, :], mate)
    ebb[my192, :] = jnp.transpose(eb[...], (1, 0, 2)).reshape(ROWS, CHI)
    y_eb = rcopy(ebb.at[my192, :], ebb.at[my192, :], mate)

    def forward(name, m):
        for flow, sign, to, last in ((pr, -1, right, "own"), (ql, 1, left, "oth")):
            if (name, m) not in flow:
                continue
            flow[name, m].wait_recv()
            zz = zmod(sign * m)
            if name == "cu":
                if m < 4:
                    at = cu_at(zz) if m < 3 else cu_at(zz, 0 if last == "own" else 1)
                    flow[name, m + 1] = rcopy(at, at, to)
            elif m < 3 or (m == 3 and name == last):
                at = pu_at(yl if name == "own" else yo, zz)
                flow[name, m + 1] = rcopy(at, at, to)

    forward("own", 1)
    forward("cu", 1)
    size = D * D * TILE
    rowi = lax.broadcasted_iota(jnp.int32, (size, D ** 3), 0)
    coli = lax.broadcasted_iota(jnp.int32, (size, D ** 3), 1)
    legs = lax.rem(lax.div(rowi, TILE), D) * D + lax.div(rowi, D * TILE)
    weights = w[...].reshape(D ** 3, D)
    spread = jnp.zeros((size, D * D), F32)
    for l in range(D):
        one = jnp.where(coli == legs + l * D * D, 1.0, 0.0).astype(BF)
        d_at = lax.broadcasted_iota(jnp.int32, (D, D * D), 0) * D + l
        col = lax.broadcasted_iota(jnp.int32, (D, D * D), 1)
        spread = spread + mul(mul(one, weights).astype(BF), jnp.where(col == d_at, 1.0, 0.0).astype(BF))
    leg = lax.broadcasted_iota(jnp.int32, (D * D, size), 0)
    pos = lax.broadcasted_iota(jnp.int32, (D * D, size), 1)
    expand = jnp.where(leg == lax.div(pos, TILE), 1.0, 0.0).astype(BF)
    full = mul(spread.astype(BF), expand)
    inrow = lax.rem(lax.broadcasted_iota(jnp.int32, (size, 1), 0), TILE)
    incol = lax.rem(lax.broadcasted_iota(jnp.int32, (1, size), 1), TILE)
    mix[...] = jnp.where(inrow == incol, full, 0.0).astype(BF)

    forward("oth", 1)
    forward("cu", 2)
    forward("own", 2)
    forward("oth", 2)
    x_same.wait_recv()
    x_other.wait_recv()
    lpt[...] = lpb[...].T
    lane = lax.broadcasted_iota(jnp.int32, (1, HALF), 1)
    second = jnp.where(lane >= ROWS, 1, 0)
    rest = lane - second * ROWS
    target = 3 * 2 * BLK + second * BLK + rest + lax.div(rest, BLK) * (HALF - BLK)
    pick[...] = jnp.where(
        lax.broadcasted_iota(jnp.int32, pick.shape, 0) == target, 1.0, 0.0
    ).astype(BF)

    forward("cu", 3)
    forward("own", 3)
    forward("oth", 3)
    keep.wait()
    y_et.wait_recv()
    forward("cu", 4)
    e2[...] = mul(cug[...], etb[...].reshape(HALF, CHI), 1, 1).astype(BF).reshape(ZN, BLK, HALF)

    def er_at(half, q):
        return er.at[half, :, pl.ds(pl.multiple_of(q * HALF, 128), HALF)]

    def exchange(dz):
        return pltpu.make_async_remote_copy(
            src_ref=e2.at[zmod(dz)], dst_ref=er_at(yl, zq), send_sem=asem.at[min(dz, 1)], recv_sem=bsem,
            device_id=at_bond(zh, zmod(dz)), device_id_type=MESH,
        )

    for dz in (4, 3, 5, 2, 6, 1, 7):
        exchange(dz).start()

    @pl.when(zh == yl)
    def _():
        pltpu.make_async_copy(e2.at[z], er_at(yl, zq), bsem).start()

    @pl.when(zh != yl)
    def _():
        exchange(0).start()

    forward("own", 4)
    forward("oth", 4)
    y_el.wait_recv()
    y_cd.wait_recv()

    for d in range(D):
        x = mul(elb[...], pug[d]).astype(BF)
        for h in range(YN):
            for l in range(D):
                for c in range(BLK // TILE):
                    row = h * ROWS + l * BLK + c * TILE
                    to = (d * D + l) * TILE
                    xb[h, c, to:to + TILE, :] = x[row:row + TILE]
    for h in range(YN):
        for c in range(BLK // TILE):
            f = mul(mix[...], xb[h, c]).astype(BF)
            for i in range(CUTS):
                for r in range(D):
                    for u in range(D):
                        row = h * ROWS + u * BLK + c * TILE
                        part = f[(r * D + u) * TILE:(r * D + u + 1) * TILE, i * LANE:(i + 1) * LANE]
                        fb[i, row:row + TILE, r * LANE:(r + 1) * LANE] = part

    def edge_step(i):
        part = mul(lpt[...], fb[i])
        for r in range(D):
            outp[i * D + r] = part[:, r * LANE:(r + 1) * LANE]

    def own(j0, n, h, zz):
        return outp[j0:j0 + n, pl.ds(pl.multiple_of(h * HALF + zz * BLK, 16), BLK), :]

    flows = {}

    def rs_first(j0, n):
        zz = zmod(4)
        for side, h, to in ((0, 0, right), (1, 1, left)):
            sbuf[side, 0, h, j0:j0 + n] = own(j0, n, h, zz).astype(BF)
            flows[j0, side, 1] = rcopy(
                sbuf.at[side, 0, h, pl.ds(j0, n)], rbuf.at[side, 0, h, pl.ds(j0, n)], to
            )

    def rs_next(j0, n, t):
        for side, sign, to in ((0, 1, right), (1, -1, left)):
            flows[j0, side, t - 1].wait_recv()
            zz = zmod(sign * (5 - t))
            for h in range(YN):
                value = own(j0, n, h, zz)
                if t > 2 or h == side:
                    value = value + rbuf[side, t - 2, h, j0:j0 + n].astype(F32)
                sbuf[side, t - 1, h, j0:j0 + n] = value.astype(BF)
            flows[j0, side, t] = rcopy(
                sbuf.at[side, t - 1, :, pl.ds(j0, n)], rbuf.at[side, t - 1, :, pl.ds(j0, n)], to
            )

    def rs_sum(j0, n, h):
        value = own(j0, n, h, z)
        for side in range(2):
            value = value + rbuf[side, 3, h, j0:j0 + n].astype(F32)
        return value.astype(BF)

    def rs_end(j0):
        for side in range(2):
            flows[j0, side, 4].wait_recv()

    def deliver(src, dst):
        return [rcopy(src.at[yl], dst, at_bond(yl, z, dx=1)), rcopy(src.at[yo], dst, at_bond(yo, z, dx=1))]

    waves = [(i * D, D) for i in range(CUTS)] + [(LOWER, CUTS), (UPPER, CUTS)]
    for i in range(CUTS):
        edge_step(i)
        rs_first(i * D, D)

    def low_step(d, carry):
        part = mul(cdb[...], pug[d]).astype(BF)
        lb[pl.ds(pl.multiple_of(d * BLK, 16), BLK), :] = part[:BLK]
        lb[pl.ds(pl.multiple_of(ROWS + d * BLK, 16), BLK), :] = part[BLK:]
        return carry

    lax.fori_loop(0, D, low_step, 0)
    y_eb.wait_recv()
    part = mul(ebb[...], lb[...], 0, 0)
    for i in range(CUTS):
        outp[LOWER + i] = part[:, i * LANE:(i + 1) * LANE]
    rs_first(LOWER, CUTS)
    rs_next(0, D, 2)
    pltpu.make_async_copy(er, er, bsem).wait()

    def pick_step(k, carry):
        shift = pl.multiple_of((3 - k) * 2 * BLK, 16)
        part = mul(er[...].reshape(YN * BLK, 4 * HALF), pick[pl.ds(shift, 4 * HALF), :]).astype(BF)
        ebuf[pl.ds(pl.multiple_of(k * BLK, 16), BLK), :] = part[:BLK]
        ebuf[pl.ds(pl.multiple_of(ROWS + k * BLK, 16), BLK), :] = part[BLK:]
        return carry

    lax.fori_loop(0, D, pick_step, 0)
    part = mul(lpt[...], ebuf[...])
    for i in range(CUTS):
        outp[UPPER + i] = part[:, i * LANE:(i + 1) * LANE]
    rs_first(UPPER, CUTS)
    for j0, n in waves[1:]:
        rs_next(j0, n, 2)
    for t in (3, 4):
        for j0, n in waves:
            rs_next(j0, n, t)
    outs = []
    for i in range(CUTS):
        rs_end(i * D)
        for h in range(YN):
            fin_edge[i, h] = jnp.transpose(rs_sum(i * D, D, h), (1, 0, 2))
        lanes = pl.ds(pl.multiple_of(yl * HALF + i * LANE, LANE), LANE)
        outs += deliver(fin_edge.at[i], edge_out.at[:, :, lanes])
    for j, (j0, dst) in enumerate((
        (LOWER, lower_out.at[:, pl.ds(pl.multiple_of(yl * HALF, LANE), HALF)]), (UPPER, upper_out.at[yl])
    )):
        rs_end(j0)
        for h in range(YN):
            total = rs_sum(j0, CUTS, h)
            for i in range(CUTS):
                fin[j, h, :, i * LANE:(i + 1) * LANE] = total[i]
        outs += deliver(fin.at[j], dst)
    rest = e2.at[pl.ds(1, ZN - 1)]
    pltpu.make_async_copy(rest, rest, asem.at[1]).wait()

    @pl.when(zh != yl)
    def _():
        exchange(0).wait_send()

    for copy in outs:
        copy.wait_recv()
    for copy in started[-SENDS:]:
        copy.wait_send()


def settle(edge_in, lower_in, upper_in, edge_out, lower_out, upper_out, edge, lower, parts, upper, sems):
    def move(i, src, dst):
        copy = pltpu.make_async_copy(src, dst, sems.at[i])
        copy.start()
        return copy

    arrived = [move(0, edge_in, edge), move(1, upper_in, parts), move(2, lower_in, lower)]
    arrived[0].wait()
    sent = [move(3, edge, edge_out)]
    arrived[1].wait()
    first, second = parts[0], parts[1]
    upper[...] = jnp.concatenate(
        [first[:, :ROWS], second[:, :ROWS], first[:, ROWS:], second[:, ROWS:]], axis=1
    )
    sent.append(move(4, upper, upper_out))
    arrived[2].wait()
    sent.append(move(5, lower, lower_out))
    for copy in sent:
        copy.wait()


def shards(
    corner_up, edge_top, edge_left, corner_down, edge_bottom, site_weights, proj_upper, proj_lower
):
    rows2 = YN * ROWS
    size = D * D * TILE
    hbm = pl.BlockSpec(memory_space=pl.ANY)
    edge, lower, upper = pl.pallas_call(
        kernel,
        out_shape=(
            jax.ShapeDtypeStruct((BLK, D, CHI), BF),
            jax.ShapeDtypeStruct((BLK, CHI), BF),
            jax.ShapeDtypeStruct((YN, BLK, HALF), BF),
        ),
        in_specs=[hbm] * 8,
        out_specs=(hbm,) * 3,
        scratch_shapes=[
            *[pltpu.VMEM((BLK, D, CHI), BF)] * 5,
            pltpu.VMEM((D, D, D, D), BF),
            pltpu.VMEM((YN, D, BLK, HALF), BF),
            pltpu.VMEM((D, CHI, HALF), BF),
            pltpu.VMEM((HALF, CHI), BF),
            pltpu.VMEM((D, YN, BLK, CHI), BF),
            pltpu.VMEM((rows2, CHI), BF),
            pltpu.VMEM((rows2, CHI), BF),
            pltpu.VMEM((rows2, CHI), BF),
            pltpu.VMEM((rows2, CHI), BF),
            pltpu.VMEM((YN * BLK, CHI), BF),
            pltpu.VMEM((size, size), BF),
            pltpu.VMEM((YN, BLK // TILE, size, HALF), BF),
            pltpu.VMEM((CUTS, rows2, D * LANE), BF),
            pltpu.VMEM((CHI, rows2), BF),
            pltpu.VMEM((rows2, HALF), BF),
            pltpu.VMEM((4 * HALF + 6 * BLK, HALF), BF),
            pltpu.VMEM((ZN, BLK, HALF), BF),
            pltpu.VMEM((YN, BLK, 4 * HALF), BF),
            pltpu.VMEM((rows2, HALF), BF),
            pltpu.VMEM((UNITS, CHI, LANE), F32),
            pltpu.VMEM((2, 4, YN, UNITS, BLK, LANE), BF),
            pltpu.VMEM((2, 4, YN, UNITS, BLK, LANE), BF),
            pltpu.VMEM((2, YN, BLK, HALF), BF),
            pltpu.VMEM((CUTS, YN, BLK, D, LANE), BF),
            pltpu.SemaphoreType.DMA((SENDS,)),
            pltpu.SemaphoreType.DMA((COPIES,)),
            pltpu.SemaphoreType.DMA((2,)),
            pltpu.SemaphoreType.DMA,
            pltpu.SemaphoreType.DMA((9,)),
        ],
        compiler_params=pltpu.CompilerParams(
            collective_id=0, has_side_effects=True, vmem_limit_bytes=56 * 1024 * 1024
        ),
    )(
        proj_upper[0, 0], proj_lower[0, 0], edge_left[0, 0], edge_top[0, 0], edge_bottom[0, 0],
        corner_up[0, 0], corner_down[0, 0], site_weights[0, 0],
    )
    edge, lower, upper = pl.pallas_call(
        settle,
        out_shape=(
            jax.ShapeDtypeStruct((BLK, D, CHI), BF),
            jax.ShapeDtypeStruct((BLK, CHI), BF),
            jax.ShapeDtypeStruct((BLK, CHI), BF),
        ),
        in_specs=[hbm] * 3,
        out_specs=(hbm,) * 3,
        scratch_shapes=[
            pltpu.VMEM((BLK, D, CHI), BF),
            pltpu.VMEM((BLK, CHI), BF),
            pltpu.VMEM((YN, BLK, HALF), BF),
            pltpu.VMEM((BLK, CHI), BF),
            pltpu.SemaphoreType.DMA((6,)),
        ],
    )(edge, lower, upper)
    return upper[None, None], edge[None, None], lower[None, None]


def solution(mesh):
    return jax.shard_map(
        shards,
        mesh=mesh,
        in_specs=(
            P("ux", "uy", "bond", None),
            P("ux", "uy", "bond", None, None),
            P("ux", "uy", "bond", None, None),
            P("ux", "uy", "bond", None),
            P("ux", "uy", "bond", None, None),
            P("ux", "uy", None, None, None, None),
            P("ux", "uy", "bond", None, None),
            P("ux", "uy", "bond", None, None),
        ),
        out_specs=(
            P("ux", "uy", "bond", None),
            P("ux", "uy", "bond", None, None),
            P("ux", "uy", "bond", None),
        ),
        check_vma=False,
    )
```

```python
import jax
import jax.numpy as jnp
from jax import lax
from jax.experimental import pallas as pl
from jax.experimental.pallas import tpu as pltpu
from jax.sharding import PartitionSpec as P

MESH = pl.DeviceIdType.MESH
BF = jnp.bfloat16
F32 = jnp.float32
ZN = 8
YN = 2
D = 4
CHI = 768
BLK = CHI // (ZN * YN)
HALF = CHI // YN
ROWS = D * BLK
LANE = 128
CUTS = HALF // LANE
TILE = 16
LOWER = CUTS * D
UPPER = LOWER + CUTS
UNITS = UPPER + CUTS
RECVS = 43
SENDS = 28


def mul(a, b, ca=1, cb=0):
    return lax.dot_general(a, b, (((ca,), (cb,)), ((), ())), preferred_element_type=F32)


def kernel(
    pu_in, low_in, el_in, et_in, eb_in, cu_in, cd_in, w_in,
    edge_out, lower_out, upper_out,
    pu, low, el, et, eb, w, put, pug, cug, etb, elb, plb, lpb, ebb, cdb, mix, xb, fb, lpt, lb, pick, e2, er, ebuf, outp, sbuf, rbuf, fin, fin_edge,
    ssem, rsem, asem, bsem, lsem,
):
    bond = lax.axis_index("bond")
    ux = lax.axis_index("ux")
    uy = lax.axis_index("uy")
    yl = lax.div(bond, ZN)
    z = lax.rem(bond, ZN)
    yo = 1 - yl
    zh = lax.div(z, ZN // 2)
    zq = lax.rem(z, ZN // 2)

    def zmod(k):
        return lax.rem(z + (k + ZN), ZN)

    def at_bond(half, zz, dx=0, dy=0):
        return (lax.rem(ux + (dx + 4), 4), lax.rem(uy + (dy + 4), 4), half * ZN + zz)

    right, left, mate = at_bond(yl, zmod(1)), at_bond(yl, zmod(-1)), at_bond(yo, z)

    my48 = pl.ds(pl.multiple_of(yl * BLK, 16), BLK)
    loads = []
    for i, (src, dst) in enumerate([
        (pu_in, pu), (cu_in, cug.at[pl.ds(pl.multiple_of(z * BLK, 16), BLK), :]), (et_in, et), (low_in, low),
        (el_in, el), (eb_in, eb), (cd_in, cdb.at[my48, :]), (w_in, w),
    ]):
        load = pltpu.make_async_copy(src, dst, lsem.at[i])
        load.start()
        loads.append(load)

    barrier = pltpu.get_barrier_semaphore()
    sources = [
        left, right, mate,
        at_bond(yl, z, dy=-1), at_bond(yo, z, dy=-1), at_bond(yl, z, dx=-1), at_bond(yo, z, dx=-1),
    ]

    def greet(to):
        pl.semaphore_signal(barrier, inc=1, device_id=to, device_id_type=MESH)

    for source in sources:
        greet(source)
    for half in range(YN):
        for q in range(ZN // 2):
            zz = yl * (ZN // 2) + q

            @pl.when(half * ZN + zz != bond)
            def _():
                greet(at_bond(half, zz))

    loads[0].wait()
    turned = jnp.transpose(pu[...], (1, 0, 2))
    put[0] = turned[:, :, :HALF]
    put[1] = turned[:, :, HALF:]
    pl.semaphore_wait(barrier, len(sources) + ZN - jnp.where(zh == yl, 1, 0))

    started = []

    used = [0]

    def fresh():
        used[0] += 1
        return rsem.at[used[0] - 1]

    def rcopy(src, dst, to, sem):
        index = len(started)
        if index >= SENDS:
            started[index - SENDS].wait_send()
        copy = pltpu.make_async_remote_copy(
            src_ref=src, dst_ref=dst, send_sem=ssem.at[index % SENDS], recv_sem=sem,
            device_id=to, device_id_type=MESH,
        )
        copy.start()
        started.append(copy)
        return copy

    def take(like, sem):
        pltpu.make_async_copy(like, like, sem).wait()

    def rows_c(half, zz):
        return pl.ds(pl.multiple_of(half * HALF + zz * BLK, 16), BLK)

    def rows_z(zz):
        return pl.ds(pl.multiple_of(zz * BLK, 16), BLK)

    my192 = pl.ds(pl.multiple_of(yl * ROWS, 16), ROWS)

    def pu_at(half, zz):
        return pug.at[:, rows_c(half, zz), :]

    def cu_at(zz, part=None):
        if part is None:
            return cug.at[rows_z(zz), :]
        return cug.at[rows_z(zz), pl.ds(part * HALF, HALF)]

    ring = {}
    for name in ("own", "oth", "cu"):
        for m in range(1, 5):
            ring[name, m] = fresh()

    def both(name, m, at_right, at_left):
        for at, to in ((at_right, right), (at_left, left)):
            if at is not None:
                rcopy(at[0], at[1], to, ring[name, m])

    both("own", 1, (put.at[yl], pu_at(yl, z)), (put.at[yl], pu_at(yl, z)))
    y_pu = rcopy(put.at[yo], pu_at(yl, z), mate, fresh())
    loads[1].wait()
    both("cu", 1, (cu_at(z), cu_at(z)), (cu_at(z), cu_at(z)))
    keep = pltpu.make_async_copy(put.at[yl], pu_at(yl, z), lsem.at[8])
    keep.start()
    for load in loads[2:]:
        load.wait()
    etb[:, yl] = jnp.transpose(et[...], (1, 0, 2))
    y_et = rcopy(etb.at[:, yl], etb.at[:, yl], mate, fresh())
    plb[my192, :] = jnp.transpose(low[...], (1, 0, 2)).reshape(ROWS, CHI)
    x_sem = fresh()
    for half in (yl, yo):
        rcopy(plb.at[my192, :], lpb.at[my192, :], at_bond(half, z, dy=1), x_sem)
    y_pu.wait_recv()
    both("oth", 1, (pu_at(yo, z), pu_at(yo, z)), (pu_at(yo, z), pu_at(yo, z)))
    elb[my192, :] = jnp.transpose(el[...], (1, 0, 2)).reshape(ROWS, CHI)
    y_el = rcopy(elb.at[my192, :], elb.at[my192, :], mate, fresh())
    y_cd = rcopy(cdb.at[my48, :], cdb.at[my48, :], mate, fresh())
    ebb[my192, :] = jnp.transpose(eb[...], (1, 0, 2)).reshape(ROWS, CHI)
    y_eb = rcopy(ebb.at[my192, :], ebb.at[my192, :], mate, fresh())

    def forward(name, m):
        if name == "cu":
            like = cug.at[pl.ds(0, BLK if m == 4 else 2 * BLK), :]
        else:
            like = put.at[0] if m == 4 else put
        take(like, ring[name, m])
        if m == 4:
            return
        if name == "cu":
            cuts = (None, None) if m < 3 else (0, 1)
            ats = [cu_at(zmod(-m), cuts[0]), cu_at(zmod(m), cuts[1])]
        else:
            half = yl if name == "own" else yo
            ats = [pu_at(half, zmod(-m)), pu_at(half, zmod(m))]
            if m == 3:
                ats[1 if name == "own" else 0] = None
        both(name, m + 1, *[None if at is None else (at, at) for at in ats])

    forward("own", 1)
    forward("cu", 1)
    size = D * D * TILE
    rowi = lax.broadcasted_iota(jnp.int32, (size, D ** 3), 0)
    coli = lax.broadcasted_iota(jnp.int32, (size, D ** 3), 1)
    legs = lax.rem(lax.div(rowi, TILE), D) * D + lax.div(rowi, D * TILE)
    weights = w[...].reshape(D ** 3, D)
    spread = jnp.zeros((size, D * D), F32)
    for l in range(D):
        one = jnp.where(coli == legs + l * D * D, 1.0, 0.0).astype(BF)
        d_at = lax.broadcasted_iota(jnp.int32, (D, D * D), 0) * D + l
        col = lax.broadcasted_iota(jnp.int32, (D, D * D), 1)
        spread = spread + mul(mul(one, weights).astype(BF), jnp.where(col == d_at, 1.0, 0.0).astype(BF))
    leg = lax.broadcasted_iota(jnp.int32, (D * D, size), 0)
    pos = lax.broadcasted_iota(jnp.int32, (D * D, size), 1)
    expand = jnp.where(leg == lax.div(pos, TILE), 1.0, 0.0).astype(BF)
    full = mul(spread.astype(BF), expand)
    inrow = lax.rem(lax.broadcasted_iota(jnp.int32, (size, 1), 0), TILE)
    incol = lax.rem(lax.broadcasted_iota(jnp.int32, (1, size), 1), TILE)
    mix[...] = jnp.where(inrow == incol, full, 0.0).astype(BF)

    forward("oth", 1)
    forward("cu", 2)
    forward("own", 2)
    forward("oth", 2)
    lane = lax.broadcasted_iota(jnp.int32, (1, HALF), 1)
    second = jnp.where(lane >= ROWS, 1, 0)
    rest = lane - second * ROWS
    target = 3 * 2 * BLK + second * BLK + rest + lax.div(rest, BLK) * (HALF - BLK)
    pick[...] = jnp.where(
        lax.broadcasted_iota(jnp.int32, pick.shape, 0) == target, 1.0, 0.0
    ).astype(BF)

    forward("cu", 3)
    forward("own", 3)
    forward("oth", 3)
    keep.wait()
    y_et.wait_recv()
    forward("cu", 4)
    e2[...] = mul(cug[...], etb[...].reshape(HALF, CHI), 1, 1).astype(BF).reshape(ZN, BLK, HALF)

    def er_at(half, q):
        return er.at[half, :, pl.ds(pl.multiple_of(q * HALF, 128), HALF)]

    def exchange(dz):
        return pltpu.make_async_remote_copy(
            src_ref=e2.at[zmod(dz)], dst_ref=er_at(yl, zq), send_sem=asem.at[min(dz, 1)], recv_sem=bsem,
            device_id=at_bond(zh, zmod(dz)), device_id_type=MESH,
        )

    for dz in (1, 7, 2, 6, 3, 5, 4):
        exchange(dz).start()

    @pl.when(zh == yl)
    def _():
        pltpu.make_async_copy(e2.at[z], er_at(yl, zq), bsem).start()

    @pl.when(zh != yl)
    def _():
        exchange(0).start()

    take(lpb, x_sem)
    lpt[...] = lpb[...].T
    forward("own", 4)
    forward("oth", 4)
    y_el.wait_recv()
    y_cd.wait_recv()

    for d in range(D):
        x = mul(elb[...], pug[d]).astype(BF)
        for h in range(YN):
            for l in range(D):
                for c in range(BLK // TILE):
                    row = h * ROWS + l * BLK + c * TILE
                    to = (d * D + l) * TILE
                    xb[h, c, to:to + TILE, :] = x[row:row + TILE]
    for h in range(YN):
        for c in range(BLK // TILE):
            f = mul(mix[...], xb[h, c]).astype(BF)
            for i in range(CUTS):
                for r in range(D):
                    for u in range(D):
                        row = h * ROWS + u * BLK + c * TILE
                        part = f[(r * D + u) * TILE:(r * D + u + 1) * TILE, i * LANE:(i + 1) * LANE]
                        fb[i, row:row + TILE, r * LANE:(r + 1) * LANE] = part

    def edge_step(i):
        part = mul(lpt[...], fb[i])
        for r in range(D):
            outp[i * D + r] = part[:, r * LANE:(r + 1) * LANE]

    def own(j0, n, h, zz):
        return outp[j0:j0 + n, pl.ds(pl.multiple_of(h * HALF + zz * BLK, 16), BLK), :]

    sums = {}

    def rs_take(j0, n, t):
        take(rbuf.at[:, t - 1, :, pl.ds(j0, n)] if t > 1 else rbuf.at[0, 0, :, pl.ds(j0, n)], sums[j0, t])

    def rs_first(j0, n):
        zz = zmod(4)
        sums[j0, 1] = fresh()
        for side, h, to in ((0, 0, right), (1, 1, left)):
            sbuf[side, 0, h, j0:j0 + n] = own(j0, n, h, zz).astype(BF)
            rcopy(
                sbuf.at[side, 0, h, pl.ds(j0, n)], rbuf.at[side, 0, h, pl.ds(j0, n)], to, sums[j0, 1]
            )

    def rs_next(j0, n, t):
        rs_take(j0, n, t - 1)
        sums[j0, t] = fresh()
        for side, sign, to in ((0, 1, right), (1, -1, left)):
            zz = zmod(sign * (5 - t))
            for h in range(YN):
                value = own(j0, n, h, zz)
                if t > 2 or h == side:
                    value = value + rbuf[side, t - 2, h, j0:j0 + n].astype(F32)
                sbuf[side, t - 1, h, j0:j0 + n] = value.astype(BF)
            rcopy(
                sbuf.at[side, t - 1, :, pl.ds(j0, n)], rbuf.at[side, t - 1, :, pl.ds(j0, n)], to, sums[j0, t]
            )

    def rs_sum(j0, n, h):
        value = own(j0, n, h, z)
        for side in range(2):
            value = value + rbuf[side, 3, h, j0:j0 + n].astype(F32)
        return value.astype(BF)

    def deliver(src, dst):
        sem = fresh()
        for half in (yl, yo):
            rcopy(src.at[half], dst, at_bond(half, z, dx=1), sem)
        return [(src, sem)]

    waves = [(i * D, D) for i in range(CUTS)] + [(LOWER, CUTS), (UPPER, CUTS)]
    for i in range(CUTS):
        edge_step(i)
        rs_first(i * D, D)

    def low_step(d, carry):
        part = mul(cdb[...], pug[d]).astype(BF)
        lb[pl.ds(pl.multiple_of(d * BLK, 16), BLK), :] = part[:BLK]
        lb[pl.ds(pl.multiple_of(ROWS + d * BLK, 16), BLK), :] = part[BLK:]
        return carry

    lax.fori_loop(0, D, low_step, 0)
    y_eb.wait_recv()
    part = mul(ebb[...], lb[...], 0, 0)
    for i in range(CUTS):
        outp[LOWER + i] = part[:, i * LANE:(i + 1) * LANE]
    rs_first(LOWER, CUTS)
    rs_next(0, D, 2)
    pltpu.make_async_copy(er, er, bsem).wait()

    def pick_step(k, carry):
        shift = pl.multiple_of((3 - k) * 2 * BLK, 16)
        part = mul(er[...].reshape(YN * BLK, 4 * HALF), pick[pl.ds(shift, 4 * HALF), :]).astype(BF)
        ebuf[pl.ds(pl.multiple_of(k * BLK, 16), BLK), :] = part[:BLK]
        ebuf[pl.ds(pl.multiple_of(ROWS + k * BLK, 16), BLK), :] = part[BLK:]
        return carry

    lax.fori_loop(0, D, pick_step, 0)
    part = mul(lpt[...], ebuf[...])
    for i in range(CUTS):
        outp[UPPER + i] = part[:, i * LANE:(i + 1) * LANE]
    rs_first(UPPER, CUTS)
    for j0, n in waves[1:]:
        rs_next(j0, n, 2)
    for t in (3, 4):
        for j0, n in waves:
            rs_next(j0, n, t)
    outs = []
    for i in range(CUTS):
        rs_take(i * D, D, 4)
        for h in range(YN):
            fin_edge[i, h] = jnp.transpose(rs_sum(i * D, D, h), (1, 0, 2))
        lanes = pl.ds(pl.multiple_of(yl * HALF + i * LANE, LANE), LANE)
        outs += deliver(fin_edge.at[i], edge_out.at[:, :, lanes])
    for j, (j0, dst) in enumerate((
        (LOWER, lower_out.at[:, pl.ds(pl.multiple_of(yl * HALF, LANE), HALF)]), (UPPER, upper_out.at[yl])
    )):
        rs_take(j0, CUTS, 4)
        for h in range(YN):
            total = rs_sum(j0, CUTS, h)
            for i in range(CUTS):
                fin[j, h, :, i * LANE:(i + 1) * LANE] = total[i]
        outs += deliver(fin.at[j], dst)
    rest = e2.at[pl.ds(1, ZN - 1)]
    pltpu.make_async_copy(rest, rest, asem.at[1]).wait()

    @pl.when(zh != yl)
    def _():
        exchange(0).wait_send()

    for like, sem in outs:
        take(like, sem)
    for copy in started[-SENDS:]:
        copy.wait_send()


def settle(edge_in, lower_in, upper_in, edge_out, lower_out, upper_out, edge, lower, parts, upper, sems):
    def move(i, src, dst):
        copy = pltpu.make_async_copy(src, dst, sems.at[i])
        copy.start()
        return copy

    arrived = [move(0, edge_in, edge), move(1, upper_in, parts), move(2, lower_in, lower)]
    arrived[0].wait()
    sent = [move(3, edge, edge_out)]
    arrived[1].wait()
    first, second = parts[0], parts[1]
    upper[...] = jnp.concatenate(
        [first[:, :ROWS], second[:, :ROWS], first[:, ROWS:], second[:, ROWS:]], axis=1
    )
    sent.append(move(4, upper, upper_out))
    arrived[2].wait()
    sent.append(move(5, lower, lower_out))
    for copy in sent:
        copy.wait()


def shards(
    corner_up, edge_top, edge_left, corner_down, edge_bottom, site_weights, proj_upper, proj_lower
):
    rows2 = YN * ROWS
    size = D * D * TILE
    hbm = pl.BlockSpec(memory_space=pl.ANY)
    edge, lower, upper = pl.pallas_call(
        kernel,
        out_shape=(
            jax.ShapeDtypeStruct((BLK, D, CHI), BF),
            jax.ShapeDtypeStruct((BLK, CHI), BF),
            jax.ShapeDtypeStruct((YN, BLK, HALF), BF),
        ),
        in_specs=[hbm] * 8,
        out_specs=(hbm,) * 3,
        scratch_shapes=[
            *[pltpu.VMEM((BLK, D, CHI), BF)] * 5,
            pltpu.VMEM((D, D, D, D), BF),
            pltpu.VMEM((YN, D, BLK, HALF), BF),
            pltpu.VMEM((D, CHI, HALF), BF),
            pltpu.VMEM((HALF, CHI), BF),
            pltpu.VMEM((D, YN, BLK, CHI), BF),
            pltpu.VMEM((rows2, CHI), BF),
            pltpu.VMEM((rows2, CHI), BF),
            pltpu.VMEM((rows2, CHI), BF),
            pltpu.VMEM((rows2, CHI), BF),
            pltpu.VMEM((YN * BLK, CHI), BF),
            pltpu.VMEM((size, size), BF),
            pltpu.VMEM((YN, BLK // TILE, size, HALF), BF),
            pltpu.VMEM((CUTS, rows2, D * LANE), BF),
            pltpu.VMEM((CHI, rows2), BF),
            pltpu.VMEM((rows2, HALF), BF),
            pltpu.VMEM((4 * HALF + 6 * BLK, HALF), BF),
            pltpu.VMEM((ZN, BLK, HALF), BF),
            pltpu.VMEM((YN, BLK, 4 * HALF), BF),
            pltpu.VMEM((rows2, HALF), BF),
            pltpu.VMEM((UNITS, CHI, LANE), F32),
            pltpu.VMEM((2, 4, YN, UNITS, BLK, LANE), BF),
            pltpu.VMEM((2, 4, YN, UNITS, BLK, LANE), BF),
            pltpu.VMEM((2, YN, BLK, HALF), BF),
            pltpu.VMEM((CUTS, YN, BLK, D, LANE), BF),
            pltpu.SemaphoreType.DMA((SENDS,)),
            pltpu.SemaphoreType.DMA((RECVS,)),
            pltpu.SemaphoreType.DMA((2,)),
            pltpu.SemaphoreType.DMA,
            pltpu.SemaphoreType.DMA((9,)),
        ],
        compiler_params=pltpu.CompilerParams(
            collective_id=0, has_side_effects=True, vmem_limit_bytes=56 * 1024 * 1024
        ),
    )(
        proj_upper[0, 0], proj_lower[0, 0], edge_left[0, 0], edge_top[0, 0], edge_bottom[0, 0],
        corner_up[0, 0], corner_down[0, 0], site_weights[0, 0],
    )
    edge, lower, upper = pl.pallas_call(
        settle,
        out_shape=(
            jax.ShapeDtypeStruct((BLK, D, CHI), BF),
            jax.ShapeDtypeStruct((BLK, CHI), BF),
            jax.ShapeDtypeStruct((BLK, CHI), BF),
        ),
        in_specs=[hbm] * 3,
        out_specs=(hbm,) * 3,
        scratch_shapes=[
            pltpu.VMEM((BLK, D, CHI), BF),
            pltpu.VMEM((BLK, CHI), BF),
            pltpu.VMEM((YN, BLK, HALF), BF),
            pltpu.VMEM((BLK, CHI), BF),
            pltpu.SemaphoreType.DMA((6,)),
        ],
    )(edge, lower, upper)
    return upper[None, None], edge[None, None], lower[None, None]


def solution(mesh):
    return jax.shard_map(
        shards,
        mesh=mesh,
        in_specs=(
            P("ux", "uy", "bond", None),
            P("ux", "uy", "bond", None, None),
            P("ux", "uy", "bond", None, None),
            P("ux", "uy", "bond", None),
            P("ux", "uy", "bond", None, None),
            P("ux", "uy", None, None, None, None),
            P("ux", "uy", "bond", None, None),
            P("ux", "uy", "bond", None, None),
        ),
        out_specs=(
            P("ux", "uy", "bond", None),
            P("ux", "uy", "bond", None, None),
            P("ux", "uy", "bond", None),
        ),
        check_vma=False,
    )
```

```python
import jax
import jax.numpy as jnp
from jax import lax
from jax.experimental import pallas as pl
from jax.experimental.pallas import tpu as pltpu
from jax.sharding import PartitionSpec as P

MESH = pl.DeviceIdType.MESH
BF = jnp.bfloat16
F32 = jnp.float32
ZN = 8
YN = 2
D = 4
CHI = 768
BLK = CHI // (ZN * YN)
HALF = CHI // YN
ROWS = D * BLK
LANE = 128
CUTS = HALF // LANE
TILE = 16
LOWER = CUTS * D
UPPER = LOWER + CUTS
UNITS = UPPER + CUTS
RECVS = 51
SENDS = 28


def mul(a, b, ca=1, cb=0):
    return lax.dot_general(a, b, (((ca,), (cb,)), ((), ())), preferred_element_type=F32)


def kernel(
    pu_in, low_in, el_in, et_in, eb_in, cu_in, cd_in, w_in,
    edge_out, lower_out, upper_out,
    pu, low, el, et, eb, w, put, pug, cug, etb, elb, plb, lpb, ebb, cdb, mix, xb, fb, lpt, lb, pick, e2, er, ebuf, outp, sbuf, rbuf, fin, fin_edge,
    ssem, rsem, asem, bsem, lsem,
):
    bond = lax.axis_index("bond")
    ux = lax.axis_index("ux")
    uy = lax.axis_index("uy")
    yl = lax.div(bond, ZN)
    z = lax.rem(bond, ZN)
    yo = 1 - yl
    zh = lax.div(z, ZN // 2)
    zq = lax.rem(z, ZN // 2)

    def zmod(k):
        return lax.rem(z + (k + ZN), ZN)

    def at_bond(half, zz, dx=0, dy=0):
        return (lax.rem(ux + (dx + 4), 4), lax.rem(uy + (dy + 4), 4), half * ZN + zz)

    right, left, mate = at_bond(yl, zmod(1)), at_bond(yl, zmod(-1)), at_bond(yo, z)

    my48 = pl.ds(pl.multiple_of(yl * BLK, 16), BLK)
    loads = []
    for i, (src, dst) in enumerate([
        (pu_in, pu), (cu_in, cug.at[pl.ds(pl.multiple_of(z * BLK, 16), BLK), :]), (et_in, et), (low_in, low),
        (el_in, el), (eb_in, eb), (cd_in, cdb.at[my48, :]), (w_in, w),
    ]):
        load = pltpu.make_async_copy(src, dst, lsem.at[i])
        load.start()
        loads.append(load)

    barrier = pltpu.get_barrier_semaphore()
    sources = [
        left, right, mate,
        at_bond(yl, z, dy=-1), at_bond(yo, z, dy=-1), at_bond(yl, z, dx=-1), at_bond(yo, z, dx=-1),
    ]

    def greet(to):
        pl.semaphore_signal(barrier, inc=1, device_id=to, device_id_type=MESH)

    for source in sources:
        greet(source)
    for half in range(YN):
        for q in range(ZN // 2):
            zz = yl * (ZN // 2) + q

            @pl.when(half * ZN + zz != bond)
            def _():
                greet(at_bond(half, zz))

    loads[0].wait()
    turned = jnp.transpose(pu[...], (1, 0, 2))
    put[0] = turned[:, :, :HALF]
    put[1] = turned[:, :, HALF:]
    pl.semaphore_wait(barrier, len(sources) + ZN - jnp.where(zh == yl, 1, 0))

    started = []

    used = [0]

    def fresh():
        used[0] += 1
        return rsem.at[used[0] - 1]

    def rcopy(src, dst, to, sem):
        index = len(started)
        if index >= SENDS:
            started[index - SENDS].wait_send()
        copy = pltpu.make_async_remote_copy(
            src_ref=src, dst_ref=dst, send_sem=ssem.at[index % SENDS], recv_sem=sem,
            device_id=to, device_id_type=MESH,
        )
        copy.start()
        started.append(copy)
        return copy

    def take(like, sem):
        pltpu.make_async_copy(like, like, sem).wait()

    def rows_c(half, zz):
        return pl.ds(pl.multiple_of(half * HALF + zz * BLK, 16), BLK)

    def rows_z(zz):
        return pl.ds(pl.multiple_of(zz * BLK, 16), BLK)

    my192 = pl.ds(pl.multiple_of(yl * ROWS, 16), ROWS)

    def pu_at(half, zz):
        return pug.at[:, rows_c(half, zz), :]

    def cu_at(zz, part=None):
        if part is None:
            return cug.at[rows_z(zz), :]
        return cug.at[rows_z(zz), pl.ds(part * HALF, HALF)]

    ring = {}
    for name in ("own", "oth", "cu"):
        for m in range(1, 5):
            ring[name, m] = fresh()

    def both(name, m, at_right, at_left):
        for at, to in ((at_right, right), (at_left, left)):
            if at is not None:
                rcopy(at[0], at[1], to, ring[name, m])

    loads[1].wait()
    both("cu", 1, (cu_at(z), cu_at(z)), (cu_at(z), cu_at(z)))
    both("own", 1, (put.at[yl], pu_at(yl, z)), (put.at[yl], pu_at(yl, z)))
    y_pu = rcopy(put.at[yo], pu_at(yl, z), mate, fresh())
    keep = pltpu.make_async_copy(put.at[yl], pu_at(yl, z), lsem.at[8])
    keep.start()
    for load in loads[2:]:
        load.wait()
    etb[:, yl] = jnp.transpose(et[...], (1, 0, 2))
    y_et = rcopy(etb.at[:, yl], etb.at[:, yl], mate, fresh())
    plb[my192, :] = jnp.transpose(low[...], (1, 0, 2)).reshape(ROWS, CHI)
    x_sem = fresh()
    for half in (yl, yo):
        rcopy(plb.at[my192, :], lpb.at[my192, :], at_bond(half, z, dy=1), x_sem)
    y_pu.wait_recv()
    both("oth", 1, (pu_at(yo, z), pu_at(yo, z)), (pu_at(yo, z), pu_at(yo, z)))
    elb[my192, :] = jnp.transpose(el[...], (1, 0, 2)).reshape(ROWS, CHI)
    y_el = rcopy(elb.at[my192, :], elb.at[my192, :], mate, fresh())
    y_cd = rcopy(cdb.at[my48, :], cdb.at[my48, :], mate, fresh())
    ebb[my192, :] = jnp.transpose(eb[...], (1, 0, 2)).reshape(ROWS, CHI)
    y_eb = rcopy(ebb.at[my192, :], ebb.at[my192, :], mate, fresh())

    def forward(name, m):
        if name == "cu":
            like = cug.at[pl.ds(0, BLK if m == 4 else 2 * BLK), :]
        else:
            like = put.at[0] if m == 4 else put
        take(like, ring[name, m])
        if m == 4:
            return
        if name == "cu":
            cuts = (None, None) if m < 3 else (0, 1)
            ats = [cu_at(zmod(-m), cuts[0]), cu_at(zmod(m), cuts[1])]
        else:
            half = yl if name == "own" else yo
            ats = [pu_at(half, zmod(-m)), pu_at(half, zmod(m))]
            if m == 3:
                ats[1 if name == "own" else 0] = None
        both(name, m + 1, *[None if at is None else (at, at) for at in ats])

    forward("cu", 1)
    forward("own", 1)
    size = D * D * TILE
    rowi = lax.broadcasted_iota(jnp.int32, (size, D ** 3), 0)
    coli = lax.broadcasted_iota(jnp.int32, (size, D ** 3), 1)
    legs = lax.rem(lax.div(rowi, TILE), D) * D + lax.div(rowi, D * TILE)
    weights = w[...].reshape(D ** 3, D)
    spread = jnp.zeros((size, D * D), F32)
    for l in range(D):
        one = jnp.where(coli == legs + l * D * D, 1.0, 0.0).astype(BF)
        d_at = lax.broadcasted_iota(jnp.int32, (D, D * D), 0) * D + l
        col = lax.broadcasted_iota(jnp.int32, (D, D * D), 1)
        spread = spread + mul(mul(one, weights).astype(BF), jnp.where(col == d_at, 1.0, 0.0).astype(BF))
    leg = lax.broadcasted_iota(jnp.int32, (D * D, size), 0)
    pos = lax.broadcasted_iota(jnp.int32, (D * D, size), 1)
    expand = jnp.where(leg == lax.div(pos, TILE), 1.0, 0.0).astype(BF)
    full = mul(spread.astype(BF), expand)
    inrow = lax.rem(lax.broadcasted_iota(jnp.int32, (size, 1), 0), TILE)
    incol = lax.rem(lax.broadcasted_iota(jnp.int32, (1, size), 1), TILE)
    mix[...] = jnp.where(inrow == incol, full, 0.0).astype(BF)

    forward("oth", 1)
    forward("cu", 2)
    forward("own", 2)
    forward("oth", 2)
    lane = lax.broadcasted_iota(jnp.int32, (1, HALF), 1)
    second = jnp.where(lane >= ROWS, 1, 0)
    rest = lane - second * ROWS
    target = 3 * 2 * BLK + second * BLK + rest + lax.div(rest, BLK) * (HALF - BLK)
    pick[...] = jnp.where(
        lax.broadcasted_iota(jnp.int32, pick.shape, 0) == target, 1.0, 0.0
    ).astype(BF)

    forward("cu", 3)
    forward("own", 3)
    forward("oth", 3)
    keep.wait()
    y_et.wait_recv()
    forward("cu", 4)
    e2[...] = mul(cug[...], etb[...].reshape(HALF, CHI), 1, 1).astype(BF).reshape(ZN, BLK, HALF)

    def er_at(half, q):
        return er.at[half, :, pl.ds(pl.multiple_of(q * HALF, 128), HALF)]

    def exchange(dz):
        return pltpu.make_async_remote_copy(
            src_ref=e2.at[zmod(dz)], dst_ref=er_at(yl, zq), send_sem=asem.at[min(dz, 1)], recv_sem=bsem,
            device_id=at_bond(zh, zmod(dz)), device_id_type=MESH,
        )

    for dz in (1, 7, 2, 6, 3, 5, 4):
        exchange(dz).start()

    @pl.when(zh == yl)
    def _():
        pltpu.make_async_copy(e2.at[z], er_at(yl, zq), bsem).start()

    @pl.when(zh != yl)
    def _():
        exchange(0).start()

    take(lpb, x_sem)
    lpt[...] = lpb[...].T
    forward("own", 4)
    forward("oth", 4)
    y_el.wait_recv()
    y_cd.wait_recv()

    for d in range(D):
        x = mul(elb[...], pug[d]).astype(BF)
        for h in range(YN):
            for l in range(D):
                for c in range(BLK // TILE):
                    row = h * ROWS + l * BLK + c * TILE
                    to = (d * D + l) * TILE
                    xb[h, c, to:to + TILE, :] = x[row:row + TILE]
    for h in range(YN):
        for c in range(BLK // TILE):
            f = mul(mix[...], xb[h, c]).astype(BF)
            for i in range(CUTS):
                for r in range(D):
                    for u in range(D):
                        row = h * ROWS + u * BLK + c * TILE
                        part = f[(r * D + u) * TILE:(r * D + u + 1) * TILE, i * LANE:(i + 1) * LANE]
                        fb[i, row:row + TILE, r * LANE:(r + 1) * LANE] = part

    def edge_step(i):
        part = mul(lpt[...], fb[i])
        for r in range(D):
            outp[i * D + r] = part[:, r * LANE:(r + 1) * LANE]

    def own(j0, n, h, zz):
        return outp[j0:j0 + n, pl.ds(pl.multiple_of(h * HALF + zz * BLK, 16), BLK), :]

    sums = {}

    def rs_take(j0, n, t):
        take(rbuf.at[:, t - 1, :, pl.ds(j0, n)] if t > 1 else rbuf.at[0, 0, :, pl.ds(j0, n)], sums[j0, t])

    def rs_first(j0, n):
        zz = zmod(4)
        sums[j0, 1] = fresh()
        for side, h, to in ((0, 0, right), (1, 1, left)):
            sbuf[side, 0, h, j0:j0 + n] = own(j0, n, h, zz).astype(BF)
            rcopy(
                sbuf.at[side, 0, h, pl.ds(j0, n)], rbuf.at[side, 0, h, pl.ds(j0, n)], to, sums[j0, 1]
            )

    def rs_next(j0, n, t, taken=False):
        if not taken:
            rs_take(j0, n, t - 1)
        sums[j0, t] = fresh()
        for side, sign, to in ((0, 1, right), (1, -1, left)):
            zz = zmod(sign * (5 - t))
            for h in range(YN):
                value = own(j0, n, h, zz)
                if t > 2 or h == side:
                    value = value + rbuf[side, t - 2, h, j0:j0 + n].astype(F32)
                sbuf[side, t - 1, h, j0:j0 + n] = value.astype(BF)
            rcopy(
                sbuf.at[side, t - 1, :, pl.ds(j0, n)], rbuf.at[side, t - 1, :, pl.ds(j0, n)], to, sums[j0, t]
            )

    def rs_sum(j0, n, h):
        value = own(j0, n, h, z)
        for side in range(2):
            value = value + rbuf[side, 3, h, j0:j0 + n].astype(F32)
        return value.astype(BF)

    def deliver(src, dst):
        sem = fresh()
        for half in (yl, yo):
            rcopy(src.at[half], dst, at_bond(half, z, dx=1), sem)
        return [(src, sem)]

    waves = [(i * D, D) for i in range(CUTS)] + [(LOWER, CUTS), (UPPER, CUTS)]
    for i in range(CUTS):
        edge_step(i)
        rs_first(i * D, D)

    def low_step(d, carry):
        part = mul(cdb[...], pug[d]).astype(BF)
        lb[pl.ds(pl.multiple_of(d * BLK, 16), BLK), :] = part[:BLK]
        lb[pl.ds(pl.multiple_of(ROWS + d * BLK, 16), BLK), :] = part[BLK:]
        return carry

    lax.fori_loop(0, D, low_step, 0)
    y_eb.wait_recv()
    part = mul(ebb[...], lb[...], 0, 0)
    for i in range(CUTS):
        outp[LOWER + i] = part[:, i * LANE:(i + 1) * LANE]
    rs_first(LOWER, CUTS)
    rs_next(0, D, 2)
    pltpu.make_async_copy(er, er, bsem).wait()

    def pick_step(k, carry):
        shift = pl.multiple_of((3 - k) * 2 * BLK, 16)
        part = mul(er[...].reshape(YN * BLK, 4 * HALF), pick[pl.ds(shift, 4 * HALF), :]).astype(BF)
        ebuf[pl.ds(pl.multiple_of(k * BLK, 16), BLK), :] = part[:BLK]
        ebuf[pl.ds(pl.multiple_of(ROWS + k * BLK, 16), BLK), :] = part[BLK:]
        return carry

    lax.fori_loop(0, D, pick_step, 0)
    part = mul(lpt[...], ebuf[...])
    for i in range(CUTS):
        outp[UPPER + i] = part[:, i * LANE:(i + 1) * LANE]
    rs_first(UPPER, CUTS)
    for j0, n in waves[1:]:
        rs_next(j0, n, 2)
    for j0, n in waves:
        rs_next(j0, n, 3)
    for i in range(CUTS):
        rs_next(i * D, D, 4)
    for j0 in (LOWER, UPPER):
        rs_take(j0, CUTS, 3)
        for i in range(CUTS):
            rs_next(j0 + i, 1, 4, taken=True)
    outs = []
    for i in range(CUTS):
        rs_take(i * D, D, 4)
        for h in range(YN):
            fin_edge[i, h] = jnp.transpose(rs_sum(i * D, D, h), (1, 0, 2))
        lanes = pl.ds(pl.multiple_of(yl * HALF + i * LANE, LANE), LANE)
        outs += deliver(fin_edge.at[i], edge_out.at[:, :, lanes])
    for j, j0 in enumerate((LOWER, UPPER)):
        for i in range(CUTS):
            rs_take(j0 + i, 1, 4)
            cut = pl.ds(i * LANE, LANE)
            for h in range(YN):
                fin[j, h, :, cut] = rs_sum(j0 + i, 1, h)[0]
            if j == 0:
                dst = lower_out.at[:, pl.ds(pl.multiple_of(yl * HALF + i * LANE, LANE), LANE)]
            else:
                dst = upper_out.at[yl, :, cut]
            outs += deliver(fin.at[j, :, :, cut], dst)
    rest = e2.at[pl.ds(1, ZN - 1)]
    pltpu.make_async_copy(rest, rest, asem.at[1]).wait()

    @pl.when(zh != yl)
    def _():
        exchange(0).wait_send()

    for like, sem in outs:
        take(like, sem)
    for copy in started[-SENDS:]:
        copy.wait_send()


def settle(edge_in, lower_in, upper_in, edge_out, lower_out, upper_out, edge, lower, parts, upper, sems):
    def move(i, src, dst):
        copy = pltpu.make_async_copy(src, dst, sems.at[i])
        copy.start()
        return copy

    arrived = [move(0, edge_in, edge), move(1, upper_in, parts), move(2, lower_in, lower)]
    arrived[0].wait()
    sent = [move(3, edge, edge_out)]
    arrived[1].wait()
    first, second = parts[0], parts[1]
    upper[...] = jnp.concatenate(
        [first[:, :ROWS], second[:, :ROWS], first[:, ROWS:], second[:, ROWS:]], axis=1
    )
    sent.append(move(4, upper, upper_out))
    arrived[2].wait()
    sent.append(move(5, lower, lower_out))
    for copy in sent:
        copy.wait()


def shards(
    corner_up, edge_top, edge_left, corner_down, edge_bottom, site_weights, proj_upper, proj_lower
):
    rows2 = YN * ROWS
    size = D * D * TILE
    hbm = pl.BlockSpec(memory_space=pl.ANY)
    edge, lower, upper = pl.pallas_call(
        kernel,
        out_shape=(
            jax.ShapeDtypeStruct((BLK, D, CHI), BF),
            jax.ShapeDtypeStruct((BLK, CHI), BF),
            jax.ShapeDtypeStruct((YN, BLK, HALF), BF),
        ),
        in_specs=[hbm] * 8,
        out_specs=(hbm,) * 3,
        scratch_shapes=[
            *[pltpu.VMEM((BLK, D, CHI), BF)] * 5,
            pltpu.VMEM((D, D, D, D), BF),
            pltpu.VMEM((YN, D, BLK, HALF), BF),
            pltpu.VMEM((D, CHI, HALF), BF),
            pltpu.VMEM((HALF, CHI), BF),
            pltpu.VMEM((D, YN, BLK, CHI), BF),
            pltpu.VMEM((rows2, CHI), BF),
            pltpu.VMEM((rows2, CHI), BF),
            pltpu.VMEM((rows2, CHI), BF),
            pltpu.VMEM((rows2, CHI), BF),
            pltpu.VMEM((YN * BLK, CHI), BF),
            pltpu.VMEM((size, size), BF),
            pltpu.VMEM((YN, BLK // TILE, size, HALF), BF),
            pltpu.VMEM((CUTS, rows2, D * LANE), BF),
            pltpu.VMEM((CHI, rows2), BF),
            pltpu.VMEM((rows2, HALF), BF),
            pltpu.VMEM((4 * HALF + 6 * BLK, HALF), BF),
            pltpu.VMEM((ZN, BLK, HALF), BF),
            pltpu.VMEM((YN, BLK, 4 * HALF), BF),
            pltpu.VMEM((rows2, HALF), BF),
            pltpu.VMEM((UNITS, CHI, LANE), F32),
            pltpu.VMEM((2, 4, YN, UNITS, BLK, LANE), BF),
            pltpu.VMEM((2, 4, YN, UNITS, BLK, LANE), BF),
            pltpu.VMEM((2, YN, BLK, HALF), BF),
            pltpu.VMEM((CUTS, YN, BLK, D, LANE), BF),
            pltpu.SemaphoreType.DMA((SENDS,)),
            pltpu.SemaphoreType.DMA((RECVS,)),
            pltpu.SemaphoreType.DMA((2,)),
            pltpu.SemaphoreType.DMA,
            pltpu.SemaphoreType.DMA((9,)),
        ],
        compiler_params=pltpu.CompilerParams(
            collective_id=0, has_side_effects=True, vmem_limit_bytes=56 * 1024 * 1024
        ),
    )(
        proj_upper[0, 0], proj_lower[0, 0], edge_left[0, 0], edge_top[0, 0], edge_bottom[0, 0],
        corner_up[0, 0], corner_down[0, 0], site_weights[0, 0],
    )
    edge, lower, upper = pl.pallas_call(
        settle,
        out_shape=(
            jax.ShapeDtypeStruct((BLK, D, CHI), BF),
            jax.ShapeDtypeStruct((BLK, CHI), BF),
            jax.ShapeDtypeStruct((BLK, CHI), BF),
        ),
        in_specs=[hbm] * 3,
        out_specs=(hbm,) * 3,
        scratch_shapes=[
            pltpu.VMEM((BLK, D, CHI), BF),
            pltpu.VMEM((BLK, CHI), BF),
            pltpu.VMEM((YN, BLK, HALF), BF),
            pltpu.VMEM((BLK, CHI), BF),
            pltpu.SemaphoreType.DMA((6,)),
        ],
    )(edge, lower, upper)
    return upper[None, None], edge[None, None], lower[None, None]


def solution(mesh):
    return jax.shard_map(
        shards,
        mesh=mesh,
        in_specs=(
            P("ux", "uy", "bond", None),
            P("ux", "uy", "bond", None, None),
            P("ux", "uy", "bond", None, None),
            P("ux", "uy", "bond", None),
            P("ux", "uy", "bond", None, None),
            P("ux", "uy", None, None, None, None),
            P("ux", "uy", "bond", None, None),
            P("ux", "uy", "bond", None, None),
        ),
        out_specs=(
            P("ux", "uy", "bond", None),
            P("ux", "uy", "bond", None, None),
            P("ux", "uy", "bond", None),
        ),
        check_vma=False,
    )
```

```python
import jax
import jax.numpy as jnp
from jax import lax
from jax.experimental import pallas as pl
from jax.experimental.pallas import tpu as pltpu
from jax.sharding import PartitionSpec as P

MESH = pl.DeviceIdType.MESH
BF = jnp.bfloat16
F32 = jnp.float32
ZN = 8
YN = 2
D = 4
CHI = 768
BLK = CHI // (ZN * YN)
HALF = CHI // YN
ROWS = D * BLK
LANE = 128
CUTS = HALF // LANE
TILE = 16
LOWER = CUTS * D
UPPER = LOWER + CUTS
UNITS = UPPER + CUTS
RECVS = 51
SENDS = 28


def mul(a, b, ca=1, cb=0):
    return lax.dot_general(a, b, (((ca,), (cb,)), ((), ())), preferred_element_type=F32)


def kernel(
    pu_in, low_in, el_in, et_in, eb_in, cu_in, cd_in, w_in,
    edge_out, lower_out, upper_out,
    pu, low, el, et, eb, w, put, pug, cug, etb, elb, plb, lpb, ebb, cdb, mix, xb, fb, lpt, lb, pick, e2, er, ebuf, outp, sbuf, rbuf, fin, fin_edge,
    ssem, rsem, asem, bsem, lsem,
):
    bond = lax.axis_index("bond")
    ux = lax.axis_index("ux")
    uy = lax.axis_index("uy")
    yl = lax.div(bond, ZN)
    z = lax.rem(bond, ZN)
    yo = 1 - yl
    zh = lax.div(z, ZN // 2)
    zq = lax.rem(z, ZN // 2)

    def zmod(k):
        return lax.rem(z + (k + ZN), ZN)

    def at_bond(half, zz, dx=0, dy=0):
        return (lax.rem(ux + (dx + 4), 4), lax.rem(uy + (dy + 4), 4), half * ZN + zz)

    right, left, mate = at_bond(yl, zmod(1)), at_bond(yl, zmod(-1)), at_bond(yo, z)

    my48 = pl.ds(pl.multiple_of(yl * BLK, 16), BLK)
    loads = []
    for i, (src, dst) in enumerate([
        (pu_in, pu), (cu_in, cug.at[pl.ds(pl.multiple_of(z * BLK, 16), BLK), :]), (et_in, et), (low_in, low),
        (el_in, el), (eb_in, eb), (cd_in, cdb.at[my48, :]), (w_in, w),
    ]):
        load = pltpu.make_async_copy(src, dst, lsem.at[i])
        load.start()
        loads.append(load)

    barrier = pltpu.get_barrier_semaphore()
    sources = [
        left, right, mate,
        at_bond(yl, z, dy=-1), at_bond(yo, z, dy=-1), at_bond(yl, z, dx=-1), at_bond(yo, z, dx=-1),
    ]

    def greet(to):
        pl.semaphore_signal(barrier, inc=1, device_id=to, device_id_type=MESH)

    for source in sources:
        greet(source)
    for k in range(ZN // 2):
        zz = yl * (ZN // 2) + lax.rem(zq + k, ZN // 2)
        greet(at_bond(yo, zz))
        if k:
            greet(at_bond(yl, zz))

    @pl.when(zh != yl)
    def _():
        greet(at_bond(yl, yl * (ZN // 2) + zq))

    loads[0].wait()
    turned = jnp.transpose(pu[...], (1, 0, 2))
    put[0] = turned[:, :, :HALF]
    put[1] = turned[:, :, HALF:]
    pl.semaphore_wait(barrier, len(sources) + ZN - jnp.where(zh == yl, 1, 0))

    started = []

    used = [0]

    def fresh():
        used[0] += 1
        return rsem.at[used[0] - 1]

    def rcopy(src, dst, to, sem):
        index = len(started)
        if index >= SENDS:
            started[index - SENDS].wait_send()
        copy = pltpu.make_async_remote_copy(
            src_ref=src, dst_ref=dst, send_sem=ssem.at[index % SENDS], recv_sem=sem,
            device_id=to, device_id_type=MESH,
        )
        copy.start()
        started.append(copy)
        return copy

    def take(like, sem):
        pltpu.make_async_copy(like, like, sem).wait()

    def rows_c(half, zz):
        return pl.ds(pl.multiple_of(half * HALF + zz * BLK, 16), BLK)

    def rows_z(zz):
        return pl.ds(pl.multiple_of(zz * BLK, 16), BLK)

    my192 = pl.ds(pl.multiple_of(yl * ROWS, 16), ROWS)

    def pu_at(half, zz):
        return pug.at[:, rows_c(half, zz), :]

    def cu_at(zz, part=None):
        if part is None:
            return cug.at[rows_z(zz), :]
        return cug.at[rows_z(zz), pl.ds(part * HALF, HALF)]

    ring = {}
    for name in ("own", "oth", "cu"):
        for m in range(1, 5):
            ring[name, m] = fresh()

    def both(name, m, at_right, at_left):
        for at, to in ((at_right, right), (at_left, left)):
            if at is not None:
                rcopy(at[0], at[1], to, ring[name, m])

    loads[1].wait()
    both("cu", 1, (cu_at(z), cu_at(z)), (cu_at(z), cu_at(z)))
    both("own", 1, (put.at[yl], pu_at(yl, z)), (put.at[yl], pu_at(yl, z)))
    y_pu = rcopy(put.at[yo], pu_at(yl, z), mate, fresh())
    keep = pltpu.make_async_copy(put.at[yl], pu_at(yl, z), lsem.at[8])
    keep.start()
    for load in loads[2:]:
        load.wait()
    etb[:, yl] = jnp.transpose(et[...], (1, 0, 2))
    y_et = rcopy(etb.at[:, yl], etb.at[:, yl], mate, fresh())
    plb[my192, :] = jnp.transpose(low[...], (1, 0, 2)).reshape(ROWS, CHI)
    x_sem = fresh()
    for half in (yl, yo):
        rcopy(plb.at[my192, :], lpb.at[my192, :], at_bond(half, z, dy=1), x_sem)
    y_pu.wait_recv()
    both("oth", 1, (pu_at(yo, z), pu_at(yo, z)), (pu_at(yo, z), pu_at(yo, z)))
    elb[my192, :] = jnp.transpose(el[...], (1, 0, 2)).reshape(ROWS, CHI)
    y_el = rcopy(elb.at[my192, :], elb.at[my192, :], mate, fresh())
    y_cd = rcopy(cdb.at[my48, :], cdb.at[my48, :], mate, fresh())
    ebb[my192, :] = jnp.transpose(eb[...], (1, 0, 2)).reshape(ROWS, CHI)
    y_eb = rcopy(ebb.at[my192, :], ebb.at[my192, :], mate, fresh())

    def forward(name, m):
        if name == "cu":
            like = cug.at[pl.ds(0, BLK if m == 4 else 2 * BLK), :]
        else:
            like = put.at[0] if m == 4 else put
        take(like, ring[name, m])
        if m == 4:
            return
        if name == "cu":
            cuts = (None, None) if m < 3 else (0, 1)
            ats = [cu_at(zmod(-m), cuts[0]), cu_at(zmod(m), cuts[1])]
        else:
            half = yl if name == "own" else yo
            ats = [pu_at(half, zmod(-m)), pu_at(half, zmod(m))]
            if m == 3:
                ats[1 if name == "own" else 0] = None
        both(name, m + 1, *[None if at is None else (at, at) for at in ats])

    forward("cu", 1)
    forward("own", 1)
    size = D * D * TILE
    rowi = lax.broadcasted_iota(jnp.int32, (size, D ** 3), 0)
    coli = lax.broadcasted_iota(jnp.int32, (size, D ** 3), 1)
    legs = lax.rem(lax.div(rowi, TILE), D) * D + lax.div(rowi, D * TILE)
    weights = w[...].reshape(D ** 3, D)
    spread = jnp.zeros((size, D * D), F32)
    for l in range(D):
        one = jnp.where(coli == legs + l * D * D, 1.0, 0.0).astype(BF)
        d_at = lax.broadcasted_iota(jnp.int32, (D, D * D), 0) * D + l
        col = lax.broadcasted_iota(jnp.int32, (D, D * D), 1)
        spread = spread + mul(mul(one, weights).astype(BF), jnp.where(col == d_at, 1.0, 0.0).astype(BF))
    leg = lax.broadcasted_iota(jnp.int32, (D * D, size), 0)
    pos = lax.broadcasted_iota(jnp.int32, (D * D, size), 1)
    expand = jnp.where(leg == lax.div(pos, TILE), 1.0, 0.0).astype(BF)
    full = mul(spread.astype(BF), expand)
    inrow = lax.rem(lax.broadcasted_iota(jnp.int32, (size, 1), 0), TILE)
    incol = lax.rem(lax.broadcasted_iota(jnp.int32, (1, size), 1), TILE)
    mix[...] = jnp.where(inrow == incol, full, 0.0).astype(BF)

    forward("oth", 1)
    forward("cu", 2)
    forward("own", 2)
    forward("oth", 2)
    lane = lax.broadcasted_iota(jnp.int32, (1, HALF), 1)
    second = jnp.where(lane >= ROWS, 1, 0)
    rest = lane - second * ROWS
    target = 3 * 2 * BLK + second * BLK + rest + lax.div(rest, BLK) * (HALF - BLK)
    pick[...] = jnp.where(
        lax.broadcasted_iota(jnp.int32, pick.shape, 0) == target, 1.0, 0.0
    ).astype(BF)

    forward("cu", 3)
    forward("own", 3)
    forward("oth", 3)
    keep.wait()
    y_et.wait_recv()
    forward("cu", 4)
    e2[...] = mul(cug[...], etb[...].reshape(HALF, CHI), 1, 1).astype(BF).reshape(ZN, BLK, HALF)

    def er_at(half, q):
        return er.at[half, :, pl.ds(pl.multiple_of(q * HALF, 128), HALF)]

    def exchange(dz):
        return pltpu.make_async_remote_copy(
            src_ref=e2.at[zmod(dz)], dst_ref=er_at(yl, zq), send_sem=asem.at[min(dz, 1)], recv_sem=bsem,
            device_id=at_bond(zh, zmod(dz)), device_id_type=MESH,
        )

    for dz in (1, 7, 2, 6, 3, 5, 4):
        exchange(dz).start()

    @pl.when(zh == yl)
    def _():
        pltpu.make_async_copy(e2.at[z], er_at(yl, zq), bsem).start()

    @pl.when(zh != yl)
    def _():
        exchange(0).start()

    take(lpb, x_sem)
    lpt[...] = lpb[...].T
    forward("own", 4)
    forward("oth", 4)
    y_el.wait_recv()
    y_cd.wait_recv()

    for d in range(D):
        x = mul(elb[...], pug[d]).astype(BF)
        for h in range(YN):
            for l in range(D):
                for c in range(BLK // TILE):
                    row = h * ROWS + l * BLK + c * TILE
                    to = (d * D + l) * TILE
                    xb[h, c, to:to + TILE, :] = x[row:row + TILE]
    for h in range(YN):
        for c in range(BLK // TILE):
            f = mul(mix[...], xb[h, c]).astype(BF)
            for i in range(CUTS):
                for r in range(D):
                    for u in range(D):
                        row = h * ROWS + u * BLK + c * TILE
                        part = f[(r * D + u) * TILE:(r * D + u + 1) * TILE, i * LANE:(i + 1) * LANE]
                        fb[i, row:row + TILE, r * LANE:(r + 1) * LANE] = part

    def edge_step(i):
        part = mul(lpt[...], fb[i])
        for r in range(D):
            outp[i * D + r] = part[:, r * LANE:(r + 1) * LANE]

    def own(j0, n, h, zz):
        return outp[j0:j0 + n, pl.ds(pl.multiple_of(h * HALF + zz * BLK, 16), BLK), :]

    sums = {}

    def rs_take(j0, n, t):
        take(rbuf.at[:, t - 1, :, pl.ds(j0, n)] if t > 1 else rbuf.at[0, 0, :, pl.ds(j0, n)], sums[j0, t])

    def rs_first(j0, n):
        zz = zmod(4)
        sums[j0, 1] = fresh()
        for side, h, to in ((0, 0, right), (1, 1, left)):
            sbuf[side, 0, h, j0:j0 + n] = own(j0, n, h, zz).astype(BF)
            rcopy(
                sbuf.at[side, 0, h, pl.ds(j0, n)], rbuf.at[side, 0, h, pl.ds(j0, n)], to, sums[j0, 1]
            )

    def rs_next(j0, n, t, taken=False):
        if not taken:
            rs_take(j0, n, t - 1)
        sums[j0, t] = fresh()
        for side, sign, to in ((0, 1, right), (1, -1, left)):
            zz = zmod(sign * (5 - t))
            for h in range(YN):
                value = own(j0, n, h, zz)
                if t > 2 or h == side:
                    value = value + rbuf[side, t - 2, h, j0:j0 + n].astype(F32)
                sbuf[side, t - 1, h, j0:j0 + n] = value.astype(BF)
            rcopy(
                sbuf.at[side, t - 1, :, pl.ds(j0, n)], rbuf.at[side, t - 1, :, pl.ds(j0, n)], to, sums[j0, t]
            )

    def rs_sum(j0, n, h):
        value = own(j0, n, h, z)
        for side in range(2):
            value = value + rbuf[side, 3, h, j0:j0 + n].astype(F32)
        return value.astype(BF)

    def deliver(src, dst):
        sem = fresh()
        for half in (yl, yo):
            rcopy(src.at[half], dst, at_bond(half, z, dx=1), sem)
        return [(src, sem)]

    waves = [(i * D, D) for i in range(CUTS)] + [(LOWER, CUTS), (UPPER, CUTS)]
    for i in range(CUTS):
        edge_step(i)
        rs_first(i * D, D)

    def low_step(d, carry):
        part = mul(cdb[...], pug[d]).astype(BF)
        lb[pl.ds(pl.multiple_of(d * BLK, 16), BLK), :] = part[:BLK]
        lb[pl.ds(pl.multiple_of(ROWS + d * BLK, 16), BLK), :] = part[BLK:]
        return carry

    lax.fori_loop(0, D, low_step, 0)
    y_eb.wait_recv()
    part = mul(ebb[...], lb[...], 0, 0)
    for i in range(CUTS):
        outp[LOWER + i] = part[:, i * LANE:(i + 1) * LANE]
    rs_first(LOWER, CUTS)
    rs_next(0, D, 2)
    pltpu.make_async_copy(er, er, bsem).wait()

    def pick_step(k, carry):
        shift = pl.multiple_of((3 - k) * 2 * BLK, 16)
        part = mul(er[...].reshape(YN * BLK, 4 * HALF), pick[pl.ds(shift, 4 * HALF), :]).astype(BF)
        ebuf[pl.ds(pl.multiple_of(k * BLK, 16), BLK), :] = part[:BLK]
        ebuf[pl.ds(pl.multiple_of(ROWS + k * BLK, 16), BLK), :] = part[BLK:]
        return carry

    lax.fori_loop(0, D, pick_step, 0)
    part = mul(lpt[...], ebuf[...])
    for i in range(CUTS):
        outp[UPPER + i] = part[:, i * LANE:(i + 1) * LANE]
    rs_first(UPPER, CUTS)
    for j0, n in waves[1:]:
        rs_next(j0, n, 2)
    for j0, n in waves:
        rs_next(j0, n, 3)
    for i in range(CUTS):
        rs_next(i * D, D, 4)
    for j0 in (LOWER, UPPER):
        rs_take(j0, CUTS, 3)
        for i in range(CUTS):
            rs_next(j0 + i, 1, 4, taken=True)
    outs = []
    for i in range(CUTS):
        rs_take(i * D, D, 4)
        for h in range(YN):
            fin_edge[i, h] = jnp.transpose(rs_sum(i * D, D, h), (1, 0, 2))
        lanes = pl.ds(pl.multiple_of(yl * HALF + i * LANE, LANE), LANE)
        outs += deliver(fin_edge.at[i], edge_out.at[:, :, lanes])
    for j, j0 in enumerate((LOWER, UPPER)):
        for i in range(CUTS):
            rs_take(j0 + i, 1, 4)
            cut = pl.ds(i * LANE, LANE)
            for h in range(YN):
                fin[j, h, :, cut] = rs_sum(j0 + i, 1, h)[0]
            if j == 0:
                dst = lower_out.at[:, pl.ds(pl.multiple_of(yl * HALF + i * LANE, LANE), LANE)]
            else:
                dst = upper_out.at[yl, :, cut]
            outs += deliver(fin.at[j, :, :, cut], dst)
    rest = e2.at[pl.ds(1, ZN - 1)]
    pltpu.make_async_copy(rest, rest, asem.at[1]).wait()

    @pl.when(zh != yl)
    def _():
        exchange(0).wait_send()

    for like, sem in outs:
        take(like, sem)
    for copy in started[-SENDS:]:
        copy.wait_send()


def settle(edge_in, lower_in, upper_in, edge_out, lower_out, upper_out, edge, lower, parts, upper, sems):
    def move(i, src, dst):
        copy = pltpu.make_async_copy(src, dst, sems.at[i])
        copy.start()
        return copy

    arrived = [move(0, edge_in, edge), move(1, upper_in, parts), move(2, lower_in, lower)]
    arrived[0].wait()
    sent = [move(3, edge, edge_out)]
    arrived[1].wait()
    first, second = parts[0], parts[1]
    upper[...] = jnp.concatenate(
        [first[:, :ROWS], second[:, :ROWS], first[:, ROWS:], second[:, ROWS:]], axis=1
    )
    sent.append(move(4, upper, upper_out))
    arrived[2].wait()
    sent.append(move(5, lower, lower_out))
    for copy in sent:
        copy.wait()


def shards(
    corner_up, edge_top, edge_left, corner_down, edge_bottom, site_weights, proj_upper, proj_lower
):
    rows2 = YN * ROWS
    size = D * D * TILE
    hbm = pl.BlockSpec(memory_space=pl.ANY)
    edge, lower, upper = pl.pallas_call(
        kernel,
        out_shape=(
            jax.ShapeDtypeStruct((BLK, D, CHI), BF),
            jax.ShapeDtypeStruct((BLK, CHI), BF),
            jax.ShapeDtypeStruct((YN, BLK, HALF), BF),
        ),
        in_specs=[hbm] * 8,
        out_specs=(hbm,) * 3,
        scratch_shapes=[
            *[pltpu.VMEM((BLK, D, CHI), BF)] * 5,
            pltpu.VMEM((D, D, D, D), BF),
            pltpu.VMEM((YN, D, BLK, HALF), BF),
            pltpu.VMEM((D, CHI, HALF), BF),
            pltpu.VMEM((HALF, CHI), BF),
            pltpu.VMEM((D, YN, BLK, CHI), BF),
            pltpu.VMEM((rows2, CHI), BF),
            pltpu.VMEM((rows2, CHI), BF),
            pltpu.VMEM((rows2, CHI), BF),
            pltpu.VMEM((rows2, CHI), BF),
            pltpu.VMEM((YN * BLK, CHI), BF),
            pltpu.VMEM((size, size), BF),
            pltpu.VMEM((YN, BLK // TILE, size, HALF), BF),
            pltpu.VMEM((CUTS, rows2, D * LANE), BF),
            pltpu.VMEM((CHI, rows2), BF),
            pltpu.VMEM((rows2, HALF), BF),
            pltpu.VMEM((4 * HALF + 6 * BLK, HALF), BF),
            pltpu.VMEM((ZN, BLK, HALF), BF),
            pltpu.VMEM((YN, BLK, 4 * HALF), BF),
            pltpu.VMEM((rows2, HALF), BF),
            pltpu.VMEM((UNITS, CHI, LANE), F32),
            pltpu.VMEM((2, 4, YN, UNITS, BLK, LANE), BF),
            pltpu.VMEM((2, 4, YN, UNITS, BLK, LANE), BF),
            pltpu.VMEM((2, YN, BLK, HALF), BF),
            pltpu.VMEM((CUTS, YN, BLK, D, LANE), BF),
            pltpu.SemaphoreType.DMA((SENDS,)),
            pltpu.SemaphoreType.DMA((RECVS,)),
            pltpu.SemaphoreType.DMA((2,)),
            pltpu.SemaphoreType.DMA,
            pltpu.SemaphoreType.DMA((9,)),
        ],
        compiler_params=pltpu.CompilerParams(
            collective_id=0, has_side_effects=True, vmem_limit_bytes=56 * 1024 * 1024
        ),
    )(
        proj_upper[0, 0], proj_lower[0, 0], edge_left[0, 0], edge_top[0, 0], edge_bottom[0, 0],
        corner_up[0, 0], corner_down[0, 0], site_weights[0, 0],
    )
    edge, lower, upper = pl.pallas_call(
        settle,
        out_shape=(
            jax.ShapeDtypeStruct((BLK, D, CHI), BF),
            jax.ShapeDtypeStruct((BLK, CHI), BF),
            jax.ShapeDtypeStruct((BLK, CHI), BF),
        ),
        in_specs=[hbm] * 3,
        out_specs=(hbm,) * 3,
        scratch_shapes=[
            pltpu.VMEM((BLK, D, CHI), BF),
            pltpu.VMEM((BLK, CHI), BF),
            pltpu.VMEM((YN, BLK, HALF), BF),
            pltpu.VMEM((BLK, CHI), BF),
            pltpu.SemaphoreType.DMA((6,)),
        ],
    )(edge, lower, upper)
    return upper[None, None], edge[None, None], lower[None, None]


def solution(mesh):
    return jax.shard_map(
        shards,
        mesh=mesh,
        in_specs=(
            P("ux", "uy", "bond", None),
            P("ux", "uy", "bond", None, None),
            P("ux", "uy", "bond", None, None),
            P("ux", "uy", "bond", None),
            P("ux", "uy", "bond", None, None),
            P("ux", "uy", None, None, None, None),
            P("ux", "uy", "bond", None, None),
            P("ux", "uy", "bond", None, None),
        ),
        out_specs=(
            P("ux", "uy", "bond", None),
            P("ux", "uy", "bond", None, None),
            P("ux", "uy", "bond", None),
        ),
        check_vma=False,
    )
```

```python
import jax
import jax.numpy as jnp
from jax import lax
from jax.experimental import pallas as pl
from jax.experimental.pallas import tpu as pltpu
from jax.sharding import PartitionSpec as P

MESH = pl.DeviceIdType.MESH
BF = jnp.bfloat16
F32 = jnp.float32
ZN = 8
YN = 2
D = 4
CHI = 768
BLK = CHI // (ZN * YN)
HALF = CHI // YN
ROWS = D * BLK
LANE = 128
CUTS = HALF // LANE
TILE = 16
LOWER = CUTS * D
UPPER = LOWER + CUTS
UNITS = UPPER + CUTS
RECVS = 51
SENDS = 28


def mul(a, b, ca=1, cb=0):
    return lax.dot_general(a, b, (((ca,), (cb,)), ((), ())), preferred_element_type=F32)


def kernel(
    pu_in, low_in, el_in, et_in, eb_in, cu_in, cd_in, w_in,
    edge_out, lower_out, upper_out,
    pu, low, el, et, eb, w, put, pug, cug, etb, elb, plb, lpb, ebb, cdb, mix, xb, fb, lpt, lb, pick, e2, er, ebuf, outp, sbuf, rbuf, fin, fin_edge,
    ssem, rsem, asem, bsem, lsem,
):
    bond = lax.axis_index("bond")
    ux = lax.axis_index("ux")
    uy = lax.axis_index("uy")
    yl = lax.div(bond, ZN)
    z = lax.rem(bond, ZN)
    yo = 1 - yl
    zh = lax.div(z, ZN // 2)
    zq = lax.rem(z, ZN // 2)

    def zmod(k):
        return lax.rem(z + (k + ZN), ZN)

    def at_bond(half, zz, dx=0, dy=0):
        return (lax.rem(ux + (dx + 4), 4), lax.rem(uy + (dy + 4), 4), half * ZN + zz)

    right, left, mate = at_bond(yl, zmod(1)), at_bond(yl, zmod(-1)), at_bond(yo, z)

    my48 = pl.ds(pl.multiple_of(yl * BLK, 16), BLK)
    loads = []
    for i, (src, dst) in enumerate([
        (pu_in, pu), (cu_in, cug.at[pl.ds(pl.multiple_of(z * BLK, 16), BLK), :]), (et_in, et), (low_in, low),
        (el_in, el), (eb_in, eb), (cd_in, cdb.at[my48, :]), (w_in, w),
    ]):
        load = pltpu.make_async_copy(src, dst, lsem.at[i])
        load.start()
        loads.append(load)

    barrier = pltpu.get_barrier_semaphore()
    sources = [
        left, right, mate,
        at_bond(yl, z, dy=-1), at_bond(yo, z, dy=-1), at_bond(yl, z, dx=-1), at_bond(yo, z, dx=-1),
    ]

    def greet(to):
        pl.semaphore_signal(barrier, inc=1, device_id=to, device_id_type=MESH)

    for source in sources:
        greet(source)
    for k in range(ZN // 2):
        zz = yl * (ZN // 2) + lax.rem(zq + k, ZN // 2)
        greet(at_bond(yo, zz))
        if k:
            greet(at_bond(yl, zz))

    @pl.when(zh != yl)
    def _():
        greet(at_bond(yl, yl * (ZN // 2) + zq))

    loads[0].wait()
    turned = jnp.transpose(pu[...], (1, 0, 2))
    put[0] = turned[:, :, :HALF]
    put[1] = turned[:, :, HALF:]
    pl.semaphore_wait(barrier, len(sources) + ZN - jnp.where(zh == yl, 1, 0))

    started = []

    used = [0]

    def fresh():
        used[0] += 1
        return rsem.at[used[0] - 1]

    def rcopy(src, dst, to, sem):
        index = len(started)
        if index >= SENDS:
            started[index - SENDS].wait_send()
        copy = pltpu.make_async_remote_copy(
            src_ref=src, dst_ref=dst, send_sem=ssem.at[index % SENDS], recv_sem=sem,
            device_id=to, device_id_type=MESH,
        )
        copy.start()
        started.append(copy)
        return copy

    def take(like, sem):
        pltpu.make_async_copy(like, like, sem).wait()

    def rows_c(half, zz):
        return pl.ds(pl.multiple_of(half * HALF + zz * BLK, 16), BLK)

    def rows_z(zz):
        return pl.ds(pl.multiple_of(zz * BLK, 16), BLK)

    my192 = pl.ds(pl.multiple_of(yl * ROWS, 16), ROWS)

    def pu_at(half, zz):
        return pug.at[:, rows_c(half, zz), :]

    def cu_at(zz, part=None):
        if part is None:
            return cug.at[rows_z(zz), :]
        return cug.at[rows_z(zz), pl.ds(part * HALF, HALF)]

    ring = {}
    for name in ("own", "oth", "cu"):
        for m in range(1, 5):
            ring[name, m] = fresh()

    def both(name, m, at_right, at_left):
        for at, to in ((at_right, right), (at_left, left)):
            if at is not None:
                rcopy(at[0], at[1], to, ring[name, m])

    y_pu = rcopy(put.at[yo], pu_at(yl, z), mate, fresh())
    loads[1].wait()
    both("cu", 1, (cu_at(z), cu_at(z)), (cu_at(z), cu_at(z)))
    both("own", 1, (put.at[yl], pu_at(yl, z)), (put.at[yl], pu_at(yl, z)))
    keep = pltpu.make_async_copy(put.at[yl], pu_at(yl, z), lsem.at[8])
    keep.start()
    for load in loads[2:]:
        load.wait()
    etb[:, yl] = jnp.transpose(et[...], (1, 0, 2))
    y_et = rcopy(etb.at[:, yl], etb.at[:, yl], mate, fresh())
    plb[my192, :] = jnp.transpose(low[...], (1, 0, 2)).reshape(ROWS, CHI)
    x_sem = fresh()
    for half in (yl, yo):
        rcopy(plb.at[my192, :], lpb.at[my192, :], at_bond(half, z, dy=1), x_sem)
    y_pu.wait_recv()
    both("oth", 1, (pu_at(yo, z), pu_at(yo, z)), (pu_at(yo, z), pu_at(yo, z)))
    elb[my192, :] = jnp.transpose(el[...], (1, 0, 2)).reshape(ROWS, CHI)
    y_el = rcopy(elb.at[my192, :], elb.at[my192, :], mate, fresh())
    y_cd = rcopy(cdb.at[my48, :], cdb.at[my48, :], mate, fresh())
    ebb[my192, :] = jnp.transpose(eb[...], (1, 0, 2)).reshape(ROWS, CHI)
    y_eb = rcopy(ebb.at[my192, :], ebb.at[my192, :], mate, fresh())

    def forward(name, m):
        if name == "cu":
            like = cug.at[pl.ds(0, BLK if m == 4 else 2 * BLK), :]
        else:
            like = put.at[0] if m == 4 else put
        take(like, ring[name, m])
        if m == 4:
            return
        if name == "cu":
            cuts = (None, None) if m < 3 else (0, 1)
            ats = [cu_at(zmod(-m), cuts[0]), cu_at(zmod(m), cuts[1])]
        else:
            half = yl if name == "own" else yo
            ats = [pu_at(half, zmod(-m)), pu_at(half, zmod(m))]
            if m == 3:
                ats[1 if name == "own" else 0] = None
        both(name, m + 1, *[None if at is None else (at, at) for at in ats])

    forward("cu", 1)
    forward("own", 1)
    size = D * D * TILE
    rowi = lax.broadcasted_iota(jnp.int32, (size, D ** 3), 0)
    coli = lax.broadcasted_iota(jnp.int32, (size, D ** 3), 1)
    legs = lax.rem(lax.div(rowi, TILE), D) * D + lax.div(rowi, D * TILE)
    weights = w[...].reshape(D ** 3, D)
    spread = jnp.zeros((size, D * D), F32)
    for l in range(D):
        one = jnp.where(coli == legs + l * D * D, 1.0, 0.0).astype(BF)
        d_at = lax.broadcasted_iota(jnp.int32, (D, D * D), 0) * D + l
        col = lax.broadcasted_iota(jnp.int32, (D, D * D), 1)
        spread = spread + mul(mul(one, weights).astype(BF), jnp.where(col == d_at, 1.0, 0.0).astype(BF))
    leg = lax.broadcasted_iota(jnp.int32, (D * D, size), 0)
    pos = lax.broadcasted_iota(jnp.int32, (D * D, size), 1)
    expand = jnp.where(leg == lax.div(pos, TILE), 1.0, 0.0).astype(BF)
    full = mul(spread.astype(BF), expand)
    inrow = lax.rem(lax.broadcasted_iota(jnp.int32, (size, 1), 0), TILE)
    incol = lax.rem(lax.broadcasted_iota(jnp.int32, (1, size), 1), TILE)
    mix[...] = jnp.where(inrow == incol, full, 0.0).astype(BF)

    forward("oth", 1)
    forward("cu", 2)
    forward("own", 2)
    forward("oth", 2)
    lane = lax.broadcasted_iota(jnp.int32, (1, HALF), 1)
    second = jnp.where(lane >= ROWS, 1, 0)
    rest = lane - second * ROWS
    target = 3 * 2 * BLK + second * BLK + rest + lax.div(rest, BLK) * (HALF - BLK)
    pick[...] = jnp.where(
        lax.broadcasted_iota(jnp.int32, pick.shape, 0) == target, 1.0, 0.0
    ).astype(BF)

    forward("cu", 3)
    forward("own", 3)
    forward("oth", 3)
    keep.wait()
    y_et.wait_recv()
    forward("cu", 4)
    e2[...] = mul(cug[...], etb[...].reshape(HALF, CHI), 1, 1).astype(BF).reshape(ZN, BLK, HALF)

    def er_at(half, q):
        return er.at[half, :, pl.ds(pl.multiple_of(q * HALF, 128), HALF)]

    def exchange(dz):
        return pltpu.make_async_remote_copy(
            src_ref=e2.at[zmod(dz)], dst_ref=er_at(yl, zq), send_sem=asem.at[min(dz, 1)], recv_sem=bsem,
            device_id=at_bond(zh, zmod(dz)), device_id_type=MESH,
        )

    for dz in (1, 7, 2, 6, 3, 5, 4):
        exchange(dz).start()

    @pl.when(zh == yl)
    def _():
        pltpu.make_async_copy(e2.at[z], er_at(yl, zq), bsem).start()

    @pl.when(zh != yl)
    def _():
        exchange(0).start()

    take(lpb, x_sem)
    lpt[...] = lpb[...].T
    forward("own", 4)
    forward("oth", 4)
    y_el.wait_recv()
    y_cd.wait_recv()

    for d in range(D):
        x = mul(elb[...], pug[d]).astype(BF)
        for h in range(YN):
            for l in range(D):
                for c in range(BLK // TILE):
                    row = h * ROWS + l * BLK + c * TILE
                    to = (d * D + l) * TILE
                    xb[h, c, to:to + TILE, :] = x[row:row + TILE]
    for h in range(YN):
        for c in range(BLK // TILE):
            f = mul(mix[...], xb[h, c]).astype(BF)
            for i in range(CUTS):
                for r in range(D):
                    for u in range(D):
                        row = h * ROWS + u * BLK + c * TILE
                        part = f[(r * D + u) * TILE:(r * D + u + 1) * TILE, i * LANE:(i + 1) * LANE]
                        fb[i, row:row + TILE, r * LANE:(r + 1) * LANE] = part

    def edge_step(i):
        part = mul(lpt[...], fb[i])
        for r in range(D):
            outp[i * D + r] = part[:, r * LANE:(r + 1) * LANE]

    def own(j0, n, h, zz):
        return outp[j0:j0 + n, pl.ds(pl.multiple_of(h * HALF + zz * BLK, 16), BLK), :]

    sums = {}

    def rs_take(j0, n, t):
        take(rbuf.at[:, t - 1, :, pl.ds(j0, n)] if t > 1 else rbuf.at[0, 0, :, pl.ds(j0, n)], sums[j0, t])

    def rs_first(j0, n):
        zz = zmod(4)
        sums[j0, 1] = fresh()
        for side, h, to in ((0, 0, right), (1, 1, left)):
            sbuf[side, 0, h, j0:j0 + n] = own(j0, n, h, zz).astype(BF)
            rcopy(
                sbuf.at[side, 0, h, pl.ds(j0, n)], rbuf.at[side, 0, h, pl.ds(j0, n)], to, sums[j0, 1]
            )

    def rs_next(j0, n, t, taken=False):
        if not taken:
            rs_take(j0, n, t - 1)
        sums[j0, t] = fresh()
        for side, sign, to in ((0, 1, right), (1, -1, left)):
            zz = zmod(sign * (5 - t))
            for h in range(YN):
                value = own(j0, n, h, zz)
                if t > 2 or h == side:
                    value = value + rbuf[side, t - 2, h, j0:j0 + n].astype(F32)
                sbuf[side, t - 1, h, j0:j0 + n] = value.astype(BF)
            rcopy(
                sbuf.at[side, t - 1, :, pl.ds(j0, n)], rbuf.at[side, t - 1, :, pl.ds(j0, n)], to, sums[j0, t]
            )

    def rs_sum(j0, n, h):
        value = own(j0, n, h, z)
        for side in range(2):
            value = value + rbuf[side, 3, h, j0:j0 + n].astype(F32)
        return value.astype(BF)

    def deliver(src, dst):
        sem = fresh()
        for half in (yl, yo):
            rcopy(src.at[half], dst, at_bond(half, z, dx=1), sem)
        return [(src, sem)]

    waves = [(i * D, D) for i in range(CUTS)] + [(LOWER, CUTS), (UPPER, CUTS)]
    for i in range(CUTS):
        edge_step(i)
        rs_first(i * D, D)

    def low_step(d, carry):
        part = mul(cdb[...], pug[d]).astype(BF)
        lb[pl.ds(pl.multiple_of(d * BLK, 16), BLK), :] = part[:BLK]
        lb[pl.ds(pl.multiple_of(ROWS + d * BLK, 16), BLK), :] = part[BLK:]
        return carry

    lax.fori_loop(0, D, low_step, 0)
    y_eb.wait_recv()
    part = mul(ebb[...], lb[...], 0, 0)
    for i in range(CUTS):
        outp[LOWER + i] = part[:, i * LANE:(i + 1) * LANE]
    rs_first(LOWER, CUTS)
    rs_next(0, D, 2)
    pltpu.make_async_copy(er, er, bsem).wait()

    def pick_step(k, carry):
        shift = pl.multiple_of((3 - k) * 2 * BLK, 16)
        part = mul(er[...].reshape(YN * BLK, 4 * HALF), pick[pl.ds(shift, 4 * HALF), :]).astype(BF)
        ebuf[pl.ds(pl.multiple_of(k * BLK, 16), BLK), :] = part[:BLK]
        ebuf[pl.ds(pl.multiple_of(ROWS + k * BLK, 16), BLK), :] = part[BLK:]
        return carry

    lax.fori_loop(0, D, pick_step, 0)
    part = mul(lpt[...], ebuf[...])
    for i in range(CUTS):
        outp[UPPER + i] = part[:, i * LANE:(i + 1) * LANE]
    rs_first(UPPER, CUTS)
    for j0, n in waves[1:]:
        rs_next(j0, n, 2)
    for j0, n in waves:
        rs_next(j0, n, 3)
    for i in range(CUTS):
        rs_next(i * D, D, 4)
    for j0 in (LOWER, UPPER):
        rs_take(j0, CUTS, 3)
        for i in range(CUTS):
            rs_next(j0 + i, 1, 4, taken=True)
    outs = []
    for i in range(CUTS):
        rs_take(i * D, D, 4)
        for h in range(YN):
            fin_edge[i, h] = jnp.transpose(rs_sum(i * D, D, h), (1, 0, 2))
        lanes = pl.ds(pl.multiple_of(yl * HALF + i * LANE, LANE), LANE)
        outs += deliver(fin_edge.at[i], edge_out.at[:, :, lanes])
    for j, j0 in enumerate((LOWER, UPPER)):
        for i in range(CUTS):
            rs_take(j0 + i, 1, 4)
            cut = pl.ds(i * LANE, LANE)
            for h in range(YN):
                fin[j, h, :, cut] = rs_sum(j0 + i, 1, h)[0]
            if j == 0:
                dst = lower_out.at[:, pl.ds(pl.multiple_of(yl * HALF + i * LANE, LANE), LANE)]
            else:
                dst = upper_out.at[yl, :, cut]
            outs += deliver(fin.at[j, :, :, cut], dst)
    rest = e2.at[pl.ds(1, ZN - 1)]
    pltpu.make_async_copy(rest, rest, asem.at[1]).wait()

    @pl.when(zh != yl)
    def _():
        exchange(0).wait_send()

    for like, sem in outs:
        take(like, sem)
    for copy in started[-SENDS:]:
        copy.wait_send()


def settle(edge_in, lower_in, upper_in, edge_out, lower_out, upper_out, edge, lower, parts, upper, sems):
    def move(i, src, dst):
        copy = pltpu.make_async_copy(src, dst, sems.at[i])
        copy.start()
        return copy

    arrived = [move(0, edge_in, edge), move(1, upper_in, parts), move(2, lower_in, lower)]
    arrived[0].wait()
    sent = [move(3, edge, edge_out)]
    arrived[1].wait()
    first, second = parts[0], parts[1]
    upper[...] = jnp.concatenate(
        [first[:, :ROWS], second[:, :ROWS], first[:, ROWS:], second[:, ROWS:]], axis=1
    )
    sent.append(move(4, upper, upper_out))
    arrived[2].wait()
    sent.append(move(5, lower, lower_out))
    for copy in sent:
        copy.wait()


def shards(
    corner_up, edge_top, edge_left, corner_down, edge_bottom, site_weights, proj_upper, proj_lower
):
    rows2 = YN * ROWS
    size = D * D * TILE
    hbm = pl.BlockSpec(memory_space=pl.ANY)
    edge, lower, upper = pl.pallas_call(
        kernel,
        out_shape=(
            jax.ShapeDtypeStruct((BLK, D, CHI), BF),
            jax.ShapeDtypeStruct((BLK, CHI), BF),
            jax.ShapeDtypeStruct((YN, BLK, HALF), BF),
        ),
        in_specs=[hbm] * 8,
        out_specs=(hbm,) * 3,
        scratch_shapes=[
            *[pltpu.VMEM((BLK, D, CHI), BF)] * 5,
            pltpu.VMEM((D, D, D, D), BF),
            pltpu.VMEM((YN, D, BLK, HALF), BF),
            pltpu.VMEM((D, CHI, HALF), BF),
            pltpu.VMEM((HALF, CHI), BF),
            pltpu.VMEM((D, YN, BLK, CHI), BF),
            pltpu.VMEM((rows2, CHI), BF),
            pltpu.VMEM((rows2, CHI), BF),
            pltpu.VMEM((rows2, CHI), BF),
            pltpu.VMEM((rows2, CHI), BF),
            pltpu.VMEM((YN * BLK, CHI), BF),
            pltpu.VMEM((size, size), BF),
            pltpu.VMEM((YN, BLK // TILE, size, HALF), BF),
            pltpu.VMEM((CUTS, rows2, D * LANE), BF),
            pltpu.VMEM((CHI, rows2), BF),
            pltpu.VMEM((rows2, HALF), BF),
            pltpu.VMEM((4 * HALF + 6 * BLK, HALF), BF),
            pltpu.VMEM((ZN, BLK, HALF), BF),
            pltpu.VMEM((YN, BLK, 4 * HALF), BF),
            pltpu.VMEM((rows2, HALF), BF),
            pltpu.VMEM((UNITS, CHI, LANE), F32),
            pltpu.VMEM((2, 4, YN, UNITS, BLK, LANE), BF),
            pltpu.VMEM((2, 4, YN, UNITS, BLK, LANE), BF),
            pltpu.VMEM((2, YN, BLK, HALF), BF),
            pltpu.VMEM((CUTS, YN, BLK, D, LANE), BF),
            pltpu.SemaphoreType.DMA((SENDS,)),
            pltpu.SemaphoreType.DMA((RECVS,)),
            pltpu.SemaphoreType.DMA((2,)),
            pltpu.SemaphoreType.DMA,
            pltpu.SemaphoreType.DMA((9,)),
        ],
        compiler_params=pltpu.CompilerParams(
            collective_id=0, has_side_effects=True, vmem_limit_bytes=56 * 1024 * 1024
        ),
    )(
        proj_upper[0, 0], proj_lower[0, 0], edge_left[0, 0], edge_top[0, 0], edge_bottom[0, 0],
        corner_up[0, 0], corner_down[0, 0], site_weights[0, 0],
    )
    edge, lower, upper = pl.pallas_call(
        settle,
        out_shape=(
            jax.ShapeDtypeStruct((BLK, D, CHI), BF),
            jax.ShapeDtypeStruct((BLK, CHI), BF),
            jax.ShapeDtypeStruct((BLK, CHI), BF),
        ),
        in_specs=[hbm] * 3,
        out_specs=(hbm,) * 3,
        scratch_shapes=[
            pltpu.VMEM((BLK, D, CHI), BF),
            pltpu.VMEM((BLK, CHI), BF),
            pltpu.VMEM((YN, BLK, HALF), BF),
            pltpu.VMEM((BLK, CHI), BF),
            pltpu.SemaphoreType.DMA((6,)),
        ],
    )(edge, lower, upper)
    return upper[None, None], edge[None, None], lower[None, None]


def solution(mesh):
    return jax.shard_map(
        shards,
        mesh=mesh,
        in_specs=(
            P("ux", "uy", "bond", None),
            P("ux", "uy", "bond", None, None),
            P("ux", "uy", "bond", None, None),
            P("ux", "uy", "bond", None),
            P("ux", "uy", "bond", None, None),
            P("ux", "uy", None, None, None, None),
            P("ux", "uy", "bond", None, None),
            P("ux", "uy", "bond", None, None),
        ),
        out_specs=(
            P("ux", "uy", "bond", None),
            P("ux", "uy", "bond", None, None),
            P("ux", "uy", "bond", None),
        ),
        check_vma=False,
    )
```
